256 devices in a mesh: expert: 64 (over z, y, core), cross: 4 (over x).
Axes of the slice: x: 4, y: 4, z: 8, core: 2. Of those that a mesh axis runs over, the one named last changes fastest.
Arguments:
- tokens: bfloat16 [32768, 3072], P(('expert', 'cross')), may hold values from -6 to 6
- route_ids: int32 [32768, 2], P(('expert', 'cross')), may hold values from 0 to 63, all different within a row; in each aligned block of 128 rows (0 to 127, 128 to 255, ...) at most 6 rows name the same one
- route_weight: bfloat16 [32768, 2], P(('expert', 'cross')), may hold values from 0.19921875 to 1
- cotangent: bfloat16 [32768, 3072], P(('expert', 'cross')), may hold values from -1.1953125 to 1.1953125
- up_weight: bfloat16 [64, 3072, 1024], P('expert', 'cross'), may hold values from -0.109375 to 0.109375
- down_weight: bfloat16 [64, 1024, 3072], P('expert', None, 'cross'), may hold values from -0.1875 to 0.1875
Outputs:
- d_tokens: bfloat16 [32768, 3072], P(('expert', 'cross'))
- d_route: bfloat16 [32768, 2], P(('expert', 'cross'))
- grad_up: bfloat16 [64, 3072, 1024], P('expert', 'cross')
- grad_down: bfloat16 [64, 1024, 3072], P('expert', None, 'cross')
The draws below stay inside these ranges and needn't reach their ends.
Inputs may be any that keep to these rules, and one draw needn't show every extreme that they name: `route_ids`: each row names 2 different experts. In each aligned block of 128 rows (the rows of one device) no expert is named by more than 6 rows, and in some block one expert is named by exactly 6 rows; every expert is named by some row.
All inputs are finite; a program needn't handle non-finite values.
Results may differ from the reference program's by a relative error of at most 0.015.
Values may be sent and summed in bfloat16 or wider, within the bound.
No kernel may reach another device: no remote copies, remote signals or barrier semaphores. Data moves between devices by JAX's collectives and lax.ppermute only.
A program may use at most 128 MiB of HBM per device.

```python
import math
import jax
import jax.numpy as jnp
import numpy as np
from jax import lax

D = 3072
FF = 1024
TOP = 2
TOK_DEV = 128
EXPERTS = 64
GROUPS = 4
TOKENS = 32768
CAP = 6


def steps_of(key, extent, cuts, smallest, top_value):
    def one(axis_at, parts):
        steps = jax.random.uniform(jax.random.fold_in(jax.random.fold_in(key, 6), axis_at), (parts,), jnp.float32, smallest / len(cuts), top_value / len(cuts))
        return jnp.repeat(jnp.exp(steps), extent[axis_at] // parts).reshape((-1,) + (1,) * (len(extent) - axis_at - 1))

    factor_of = one(*cuts[0])
    for cut in cuts[1:]:
        factor_of = factor_of * one(*cut)
    return factor_of


def shared_out(key, own, number, rows, number_of, top, limit, slope):
    order = jax.random.permutation(key, number_of)
    crowded, usual = portions_of(number_of, rows * top, limit, slope, True), portions_of(number_of, rows * top, limit, slope, False)
    places = jnp.arange(number_of)

    def named(lengths, offset_by):
        used = int((lengths > 0).sum())
        fixed = max(1, used // 4)
        moved = fixed + (places - fixed + offset_by * (used - fixed)) % max(1, number_of - fixed)
        return jnp.zeros((number_of,), jnp.int32).at[order[jnp.where(places < fixed, places, moved)]].set(jnp.asarray(lengths, jnp.int32))

    lengths = jnp.where(number % 4 == 0, named(crowded, number // 4), named(usual, number - number // 4 - 1))
    mixed = jax.random.permutation(jax.random.fold_in(own, 3), number_of)
    source_of, taker = mixed[0:number_of // 2 * 2:2], mixed[1:number_of // 2 * 2:2]
    slack = jnp.minimum(lengths[source_of] - 1, limit - lengths[taker]) // 2
    slack = jnp.where((source_of == order[0]) | (taker == order[0]) | (lengths[taker] == 0), 0, jnp.maximum(slack, 0))
    moved = jax.random.randint(jax.random.fold_in(own, 4), (number_of // 2,), 0, 1 << 20) % (slack + 1)
    lengths = lengths.at[source_of].add(-moved).at[taker].add(moved)
    items = jnp.searchsorted(jnp.cumsum(lengths), jnp.arange(rows * top), side="right").astype(jnp.int32)
    table = items.reshape(top, rows).T
    table = table[jax.random.permutation(jax.random.fold_in(own, 1), rows)]
    offset_by = jax.random.randint(jax.random.fold_in(own, 2), (rows, 1), 0, top)
    return jnp.take_along_axis(table, (jnp.arange(top)[None, :] + offset_by) % top, axis=1)


def portions_of(amount, total, bound, lean, full):
    weights = [(1 << 20) // math.isqrt(grade ** lean) + 1 for grade in range(1, amount + 1)]
    largest = bound if full else min(bound, max(-(-total // amount), total * weights[0] // sum(weights)))
    least = 1 if total - largest >= amount - 1 else 0
    counts, spare = [largest] + [least] * (amount - 1), total - largest - least * (amount - 1)
    while spare > 0:
        free = [i for i in range(1, amount) if counts[i] < largest] or [i for i in range(1, amount) if counts[i] < bound]
        pool, remaining = sum([weights[i] for i in free]), spare
        for i in free:
            addition = min(bound - counts[i], max(1, remaining * weights[i] // pool), spare)
            counts[i] = counts[i] + addition
            spare = spare - addition
    return np.array(counts)


def centred(rng, shape, deviation, bound, split=(), kind=jnp.bfloat16):
    result = jax.random.normal(rng, shape, jnp.float32) * deviation
    if len(split) > 0:
        result = steps_of(rng, shape, split, -0.22, 0.18) * result
    return jnp.clip(result, min=-bound, max=bound).astype(kind)


def setup_inputs(seed: int = 0) -> dict:
    keys = jax.random.split(jax.random.key(seed), 7)
    tokens = centred(keys[0], (TOKENS, D), 1.0, 6.0, ((0, 256),))
    route_ids_keys = jax.random.split(jax.random.fold_in(keys[1], 1), TOKENS // TOK_DEV)
    route_ids_turns = jax.random.permutation(jax.random.fold_in(keys[1], 3), TOKENS // TOK_DEV)
    route_ids = jax.vmap(lambda own, number: shared_out(jax.random.fold_in(keys[1], 2), own, number, TOK_DEV, EXPERTS, TOP, CAP, 2))(route_ids_keys, route_ids_turns).reshape((TOKENS, TOP))
    route_weight = jnp.clip(0.19921875 + 0.80078125 * jax.random.uniform(keys[2], (TOKENS, TOP), jnp.float32) ** steps_of(keys[2], (TOKENS, TOP), ((0, 256),), -0.2, 0.2), 0.19921875, 1.0).astype(jnp.bfloat16)
    cotangent = centred(keys[3], (TOKENS, D), 0.2, 1.1953125, ((0, 256),))
    up_weight = centred(keys[4], (EXPERTS, D, FF), D ** -0.5, 0.109375, ((0, 64), (1, 4)))
    down_weight = centred(keys[5], (EXPERTS, FF, D), FF ** -0.5, 0.1875, ((0, 64), (2, 4)))
    return dict(tokens=tokens, route_ids=route_ids, route_weight=route_weight, cotangent=cotangent, up_weight=up_weight, down_weight=down_weight)


def silu_slope(pre_act):
    sigmoid_val = jax.nn.sigmoid(pre_act)
    return sigmoid_val * (1.0 + pre_act * (1.0 - sigmoid_val))


def slot_targets(block_ids):
    flat_ids = block_ids.reshape(-1).astype(jnp.int32)
    onehot = (flat_ids[:, None] == jnp.arange(EXPERTS, dtype=jnp.int32)[None, :]).astype(jnp.int32)
    before = jnp.cumsum(onehot, axis=0) - onehot
    return (flat_ids * CAP + jnp.sum(before * onehot, axis=1)).astype(jnp.int32)


def reference(tokens, route_ids, route_weight, cotangent, up_weight, down_weight):
    block_count = EXPERTS * GROUPS
    per_block = TOK_DEV * TOP
    total_routes = TOKENS * TOP
    targets = jax.vmap(slot_targets)(route_ids.reshape(block_count, TOK_DEV, TOP))
    route_pos = jnp.broadcast_to(jnp.arange(per_block, dtype=jnp.int32)[None, :], (block_count, per_block))
    block_index = jnp.arange(block_count, dtype=jnp.int32)
    filler = jnp.full((block_count, EXPERTS * CAP), -1, jnp.int32)
    inverse = filler.at[block_index[:, None], targets].set(route_pos)
    global_route = jnp.where(inverse >= 0, block_index[:, None] * per_block + inverse, -1).astype(jnp.int32)
    flat_weight = route_weight.reshape(-1)
    rows_all = EXPERTS * CAP

    def one_expert(state_pair, expert):
        dx_routes, dr_routes = state_pair
        route_index = lax.dynamic_slice_in_dim(global_route, expert * CAP, CAP, 1)
        route_index = route_index.reshape(EXPERTS, GROUPS, CAP).transpose(1, 0, 2).reshape(GROUPS * rows_all)
        filled = route_index >= 0
        safe_index = jnp.where(filled, route_index, 0).astype(jnp.int32)
        token_index = safe_index // TOP
        zero_row = jnp.zeros((), tokens.dtype)
        expert_rows = jnp.where(filled[:, None], tokens[token_index], zero_row)
        cot_rows = jnp.where(filled[:, None], cotangent[token_index], zero_row)
        weight_rows = jnp.where(filled, flat_weight[safe_index], jnp.zeros((), flat_weight.dtype))
        up_mat = up_weight[expert]
        down_mat = down_weight[expert]
        pre_act = jnp.dot(expert_rows, up_mat, preferred_element_type=jnp.float32)
        hidden = jax.nn.silu(pre_act).astype(jnp.bfloat16)
        expert_out = jnp.dot(hidden, down_mat, preferred_element_type=jnp.float32)
        route_grad = jnp.sum(cot_rows.astype(jnp.float32) * expert_out, axis=1).astype(jnp.bfloat16)
        out_grad = (weight_rows.astype(jnp.float32)[:, None] * cot_rows.astype(jnp.float32)).astype(jnp.bfloat16)
        back_proj = jnp.dot(out_grad, down_mat.T, preferred_element_type=jnp.float32)
        hidden_grad = (back_proj * silu_slope(pre_act)).astype(jnp.bfloat16)
        input_grad = jnp.dot(hidden_grad, up_mat.T, preferred_element_type=jnp.float32).astype(jnp.bfloat16)
        scatter_at = jnp.where(filled, route_index, total_routes).astype(jnp.int32)
        dx_routes = dx_routes.at[scatter_at].set(input_grad, mode="drop")
        dr_routes = dr_routes.at[scatter_at].set(route_grad, mode="drop")
        group_rows = expert_rows.reshape(GROUPS, rows_all, D).astype(jnp.float32)
        group_hgrad = hidden_grad.reshape(GROUPS, rows_all, FF).astype(jnp.float32)
        group_hidden = hidden.reshape(GROUPS, rows_all, FF).astype(jnp.float32)
        group_ograd = out_grad.reshape(GROUPS, rows_all, D).astype(jnp.float32)
        group_up = jnp.einsum("grd,grf->gdf", group_rows, group_hgrad).astype(jnp.bfloat16)
        group_down = jnp.einsum("grf,grd->gfd", group_hidden, group_ograd).astype(jnp.bfloat16)
        grad_up_e = jnp.sum(group_up.astype(jnp.float32), axis=0).astype(jnp.bfloat16)
        grad_down_e = jnp.sum(group_down.astype(jnp.float32), axis=0).astype(jnp.bfloat16)
        return (dx_routes, dr_routes), (grad_up_e, grad_down_e)

    start_pair = (jnp.zeros((total_routes, D), jnp.bfloat16), jnp.zeros((total_routes,), jnp.bfloat16))
    final_pair, grads = lax.scan(one_expert, start_pair, jnp.arange(EXPERTS, dtype=jnp.int32))
    dx_routes, dr_routes = final_pair
    d_tokens = jnp.sum(dx_routes.reshape(TOKENS, TOP, D).astype(jnp.float32), axis=1).astype(jnp.bfloat16)
    d_route = dr_routes.reshape(TOKENS, TOP)
    return d_tokens, d_route, grads[0], grads[1]
```

```python
import functools

import jax
import jax.numpy as jnp
from jax import lax
from jax.experimental import pallas as pl
from jax.experimental.pallas import tpu as pltpu
from jax.sharding import PartitionSpec as P

CAP = 6
ROWS = 8
F32 = jnp.float32
BF16 = jnp.bfloat16
VMEM = pltpu.CompilerParams(vmem_limit_bytes=60 * 1024 * 1024)
NT = (((1,), (1,)), ((), ()))
TN = (((0,), (0,)), ((), ()))


def iota(shape, dim):
    return lax.broadcasted_iota(jnp.int32, shape, dim)


def dot(a, b, dims=None):
    if dims is None:
        return jnp.dot(a, b, preferred_element_type=F32)
    return lax.dot_general(a, b, dims, preferred_element_type=F32)


def slots(first, second):
    count = first.shape[1]
    down, across = iota((count, count), 0), iota((count, count), 1)
    eye = down == across
    earlier = (down < across).astype(F32)
    first_col = jnp.sum(jnp.where(eye, first, 0), axis=1, keepdims=True)
    second_col = jnp.sum(jnp.where(eye, second, 0), axis=1, keepdims=True)

    def total(hits):
        return jnp.sum(hits, axis=0, keepdims=True)

    rank_first = total((first_col == first).astype(F32) * earlier)
    rank_second = total((first_col == second).astype(F32)) + total(
        (second_col == second).astype(F32) * earlier
    )
    return (first, rank_first.astype(jnp.int32)), (second, rank_second.astype(jnp.int32))


def row_of(route):
    return route[0] * ROWS + route[1]


def rest_of(route):
    late = (route[1] >= 3).astype(jnp.int32)
    return route[0] * ROWS + CAP + late, route[1] - 3 * late


def chosen(hit_of, routes, shares):
    return sum(
        jnp.where(hit_of(route), share, 0.0) for route, share in zip(routes, shares)
    ).astype(BF16)


def packed_block(down, part, mine, last):
    def hit_of(route):
        row, column = rest_of(route)
        return (down == row) & (column == part)

    main = chosen(lambda route: down == row_of(route), mine[0], mine[1])
    left = jnp.concatenate([main, chosen(hit_of, last[0], last[1])], axis=1)
    return dot(left, jnp.concatenate([mine[2], last[2]], axis=0)).astype(BF16)


def block_at(place_ref, ref, delta):
    block = ref.shape[1] // 4
    start = lax.rem(place_ref[0] + delta, 4) * block
    return ref[:, pl.ds(pl.multiple_of(start, 128), block)]


def token_body(place_ref, ids_ref, values_ref, out_ref):
    count, width = values_ref.shape
    block = width // 4
    down = iota((out_ref.shape[0], count), 0)
    routes = slots(ids_ref[0:1, :], ids_ref[1:2, :])
    shares = (1.0, 1.0)
    last = (routes, shares, block_at(place_ref, values_ref, 3))
    for part in range(3):
        mine = (routes, shares, block_at(place_ref, values_ref, part))
        out_ref[:, part * block : (part + 1) * block] = packed_block(down, part, mine, last)


def dispatch_tokens(place, ids, values, experts):
    count, width = values.shape
    rows_all = experts * ROWS
    packed = 3 * width // 4
    vmem = pl.BlockSpec(memory_space=pltpu.VMEM)
    return pl.pallas_call(
        token_body,
        out_shape=jax.ShapeDtypeStruct((rows_all, packed), BF16),
        in_specs=[pl.BlockSpec(memory_space=pltpu.SMEM), vmem, vmem],
        out_specs=vmem,
        compiler_params=VMEM,
        cost_estimate=pl.CostEstimate(
            flops=4 * rows_all * count * packed,
            bytes_accessed=2 * (count * width + rows_all * packed),
            transcendentals=0,
        ),
    )(place, ids, values)


NOTES = 16


def slice_body(place_ref, ids_ref, weight_ref, values_ref, *out_refs):
    count, width = values_ref.shape
    block = width // 4
    row = iota((NOTES, count), 0)
    notes = jnp.zeros((NOTES, count), F32)
    for k in range(2):
        notes = jnp.where(row == k, ids_ref[k : k + 1, :].astype(F32), notes)
        notes = jnp.where(row == 2 + k, weight_ref[k : k + 1, :].astype(F32), notes)
    for delta, out_ref in enumerate(out_refs):
        out_ref[:count, :] = block_at(place_ref, values_ref, delta)
        out_ref[count:, :] = jnp.zeros((NOTES, block), BF16)
        out_ref[count:, :count] = notes.astype(BF16)


def slices(place, ids, weight, values):
    count, width = values.shape
    vmem = pl.BlockSpec(memory_space=pltpu.VMEM)
    return pl.pallas_call(
        slice_body,
        out_shape=[jax.ShapeDtypeStruct((count + NOTES, width // 4), BF16)] * 4,
        in_specs=[pl.BlockSpec(memory_space=pltpu.SMEM), vmem, vmem, vmem],
        out_specs=[vmem] * 4,
        compiler_params=VMEM,
        cost_estimate=pl.CostEstimate(
            flops=0, bytes_accessed=4 * count * width, transcendentals=0
        ),
    )(place, ids, weight, values)


def grad_body(s0, s1, s2, s3, out_ref):
    count = s0.shape[0] - NOTES
    block = s0.shape[1]
    down = iota((out_ref.shape[0], count), 0)
    groups = []
    for ref in (s0, s1, s2, s3):
        notes = ref[count:, :count].astype(F32)
        first, second = (notes[k : k + 1, :].astype(jnp.int32) for k in range(2))
        groups.append((slots(first, second), (notes[2:3, :], notes[3:4, :]), ref[:count, :]))
    for part in range(3):
        out_ref[:, part * block : (part + 1) * block] = packed_block(
            down, part, groups[part], groups[3]
        )


def dispatch_grads(parts, experts):
    count, block = parts[0].shape
    rows_all = experts * ROWS
    vmem = pl.BlockSpec(memory_space=pltpu.VMEM)
    return pl.pallas_call(
        grad_body,
        out_shape=jax.ShapeDtypeStruct((rows_all, 3 * block), BF16),
        in_specs=[vmem] * 4,
        out_specs=vmem,
        compiler_params=VMEM,
        cost_estimate=pl.CostEstimate(
            flops=12 * rows_all * count * block,
            bytes_accessed=2 * (4 * count + 3 * rows_all) * block,
            transcendentals=0,
        ),
    )(*parts)


def pickers(experts):
    rows, packed = experts * CAP, experts * ROWS
    at, column = iota((rows, packed), 0), iota((rows, packed), 1)
    expert = lax.shift_right_logical(at * 10923, 16)
    slot = at - expert * CAP
    late = (slot >= 3).astype(jnp.int32)
    main = (column == expert * ROWS + slot).astype(BF16)
    rest = [
        ((column == expert * ROWS + CAP + late) & (slot - 3 * late == part)).astype(BF16)
        for part in range(3)
    ]
    return main, rest


def packers(experts):
    rows, packed = experts * CAP, experts * ROWS
    at, column = iota((packed, rows), 1), iota((packed, rows), 0)
    expert = lax.shift_right_logical(at * 10923, 16)
    slot = at - expert * CAP
    late = (slot >= 3).astype(jnp.int32)
    main = (column == expert * ROWS + slot).astype(BF16)
    rest = [
        ((column == expert * ROWS + CAP + late) & (slot - 3 * late == part)).astype(BF16)
        for part in range(3)
    ]
    return main, rest


def group_size(rows_all):
    experts = rows_all // ROWS
    return min(32, experts)


def unpack(packed_ref, whole_refs):
    rows_all, packed = packed_ref.shape
    block = packed // 3
    size = group_size(rows_all)
    main, rest = pickers(size)
    for group in range(rows_all // (size * ROWS)):
        source = slice(group * size * ROWS, (group + 1) * size * ROWS)
        target = slice(group * size * CAP, (group + 1) * size * CAP)
        parts = [packed_ref[source, part * block : (part + 1) * block] for part in range(3)]
        for part in range(3):
            whole_refs[part][target, :] = dot(main, parts[part]).astype(BF16)
        whole_refs[3][target, :] = sum(dot(rest[part], parts[part]) for part in range(3)).astype(
            BF16
        )


def project_body(got_ref, down_ref, g0, g1, g2, g3, b0, b1, b2, b3):
    wholes = (g0, g1, g2, g3)
    unpack(got_ref, wholes)
    hidden_width = down_ref.shape[0]
    step = min(256, hidden_width)
    for j in range(hidden_width // step):
        at = slice(j * step, (j + 1) * step)
        weight = down_ref[at, :]
        for whole, out_ref in zip(wholes, (b0, b1, b2, b3)):
            out_ref[:, at] = dot(whole[...], weight, NT).astype(out_ref.dtype)


def project(got, down):
    rows_all, packed = got.shape
    rows = rows_all // ROWS * CAP
    block, hidden_width = packed // 3, down.shape[0]
    return pl.pallas_call(
        project_body,
        out_shape=[jax.ShapeDtypeStruct((rows, block), BF16)] * 4
        + [jax.ShapeDtypeStruct((rows, hidden_width), F32)]
        + [jax.ShapeDtypeStruct((rows, hidden_width), BF16)] * 3,
        in_specs=[pl.BlockSpec(memory_space=pltpu.VMEM)] * 2,
        out_specs=[pl.BlockSpec(memory_space=pltpu.VMEM)] * 8,
        compiler_params=VMEM,
        cost_estimate=pl.CostEstimate(
            flops=10 * rows * block * hidden_width,
            bytes_accessed=12 * rows * (block + hidden_width),
            transcendentals=0,
        ),
    )(got, down)


def hidden_body(
    got_ref, up0, up1, up2a, up2b, up3, b0, b1, b2, b3,
    x0, x1, x2, x3, hidden_ref, hgrad_ref, extra_ref,
):
    unpack(got_ref, (x0, x1, x2, x3))
    half = up2a.shape[0]
    rows, hidden_width = hidden_ref.shape
    step = min(256, hidden_width)
    score = jnp.zeros((rows, 1), F32)
    for j in range(hidden_width // step):
        at = slice(j * step, (j + 1) * step)
        pre_act = dot(x0[...], up0[:, at])
        pre_act += dot(x1[...], up1[:, at])
        pre_act += dot(x3[...], up3[:, at])
        pre_act += dot(x2[:, :half], up2a[:, at])
        pre_act += dot(x2[:, half:], up2b[:, at])
        back = b0[:, at] + b1[:, at].astype(F32) + b2[:, at].astype(F32) + b3[:, at].astype(F32)
        sigmoid_val = jax.nn.sigmoid(pre_act)
        hidden = (pre_act * sigmoid_val).astype(BF16)
        hidden_ref[:, at] = hidden
        slope = sigmoid_val * (1.0 + pre_act * (1.0 - sigmoid_val))
        hgrad_ref[:, at] = (back * slope).astype(BF16)
        score += jnp.sum(hidden.astype(F32) * back, axis=1, keepdims=True)
    high = score.astype(BF16)
    low = (score - high.astype(F32)).astype(BF16)
    lane = iota((rows, 128), 1)
    extra = jnp.where(lane == 0, high.astype(F32), jnp.where(lane == 1, low.astype(F32), 0.0))
    extra_ref[...] = extra.astype(BF16)


def hidden_grads_of(got, ups, backs):
    rows_all, packed = got.shape
    rows = rows_all // ROWS * CAP
    block, hidden_width = packed // 3, ups[0].shape[1]
    return pl.pallas_call(
        hidden_body,
        out_shape=[jax.ShapeDtypeStruct((rows, block), BF16)] * 4
        + [jax.ShapeDtypeStruct((rows, hidden_width), BF16)] * 2
        + [jax.ShapeDtypeStruct((rows, 128), BF16)],
        in_specs=[pl.BlockSpec(memory_space=pltpu.VMEM)] * 10,
        out_specs=[pl.BlockSpec(memory_space=pltpu.VMEM)] * 7,
        compiler_params=VMEM,
        cost_estimate=pl.CostEstimate(
            flops=10 * rows * block * hidden_width,
            bytes_accessed=24 * block * hidden_width,
            transcendentals=rows * hidden_width,
        ),
    )(got, *ups, *backs)


def input_body(hgrad_ref, extra_ref, up0, up1, up2a, up2b, up3, ret_ref):
    rows = hgrad_ref.shape[0]
    block = up0.shape[0]
    size = group_size(ret_ref.shape[0])
    main, rest = packers(size)
    groups = [
        (slice(g * size * CAP, (g + 1) * size * CAP), slice(g * size * ROWS, (g + 1) * size * ROWS))
        for g in range(rows // (size * CAP))
    ]
    whole = hgrad_ref[...]
    half_up = up2a.shape[0]
    chunk = min(384, half_up)
    for n in range(block // chunk):
        at = slice(n * chunk, (n + 1) * chunk)
        if (n + 1) * chunk <= half_up:
            opposite = up2a[at, :]
        else:
            opposite = up2b[n * chunk - half_up : (n + 1) * chunk - half_up, :]
        last = dot(whole, up3[at, :], NT).astype(BF16)
        for part, weight in enumerate((up0[at, :], up1[at, :], opposite)):
            here = dot(whole, weight, NT).astype(BF16)
            start = part * block + n * chunk
            for source, target in groups:
                ret_ref[target, start : start + chunk] = (
                    dot(main, here[source]) + dot(rest[part], last[source])
                ).astype(BF16)
    for source, target in groups:
        ret_ref[target, 3 * block :] = dot(main, extra_ref[source, :]).astype(BF16)


def input_grads(hgrad, extra, ups, experts):
    rows, hidden_width = hgrad.shape
    block = ups[0].shape[0]
    return pl.pallas_call(
        input_body,
        out_shape=jax.ShapeDtypeStruct((experts * ROWS, 3 * block + 128), BF16),
        in_specs=[pl.BlockSpec(memory_space=pltpu.VMEM)] * 7,
        out_specs=pl.BlockSpec(memory_space=pltpu.VMEM),
        compiler_params=VMEM,
        cost_estimate=pl.CostEstimate(
            flops=10 * rows * block * hidden_width,
            bytes_accessed=16 * block * hidden_width,
            transcendentals=0,
        ),
    )(hgrad, extra, *ups)


def combine_body(place_ref, ids_ref, weight_ref, ret_ref, dtok_ref, droute_ref):
    rows_all = ret_ref.shape[0]
    count, width = dtok_ref.shape
    block = width // 4
    routes = slots(ids_ref[0:1, :], ids_ref[1:2, :])
    eye = iota((count, count), 0) == iota((count, count), 1)

    def col(row):
        return jnp.sum(jnp.where(eye, row, jnp.zeros_like(row)), axis=1, keepdims=True)

    across = iota((count, rows_all), 1)
    hits = [(across == col(row_of(route))).astype(BF16) for route in routes]
    main = hits[0] + hits[1]
    rests = [rest_of(route) for route in routes]
    rest_rows = [col(row) for row, _ in rests]
    rest_parts = [col(part) for _, part in rests]

    def put(delta, values):
        start = lax.rem(place_ref[0] + delta, 4) * block
        dtok_ref[:, pl.ds(pl.multiple_of(start, 128), block)] = values.astype(BF16)

    last = jnp.zeros((count, block), F32)
    for part in range(3):
        got = ret_ref[:, part * block : (part + 1) * block]
        put(part, dot(main, got))
        pick = sum(
            ((across == row) & (column == part)).astype(F32)
            for row, column in zip(rest_rows, rest_parts)
        ).astype(BF16)
        last += dot(pick, got)
    put(3, last)
    extra = ret_ref[:, 3 * block :]
    lane = iota((count, 2), 1)
    out = jnp.zeros((count, 2), F32)
    for k in range(2):
        pair = dot(hits[k], extra)
        value = (pair[:, 0:1] + pair[:, 1:2]) / col(weight_ref[k : k + 1, :].astype(F32))
        out = jnp.where(lane == k, value, out)
    droute_ref[...] = out.astype(BF16)


def combine(place, ids, weight, ret, count, width):
    vmem = pl.BlockSpec(memory_space=pltpu.VMEM)
    return pl.pallas_call(
        combine_body,
        out_shape=[
            jax.ShapeDtypeStruct((count, width), BF16),
            jax.ShapeDtypeStruct((count, 2), BF16),
        ],
        in_specs=[pl.BlockSpec(memory_space=pltpu.SMEM), vmem, vmem, vmem],
        out_specs=[vmem, vmem],
        compiler_params=VMEM,
        cost_estimate=pl.CostEstimate(
            flops=4 * ret.shape[0] * count * width,
            bytes_accessed=2 * (count * width + ret.size),
            transcendentals=0,
        ),
    )(place, ids, weight, ret)


def outer_body(split_left, *refs):
    halves = refs[:5]
    wholes = refs[5:9]
    out_ref = refs[9]
    half = halves[2].shape[0]
    step = min(256, out_ref.shape[0])

    def one(j, carry):
        at = pl.ds(pl.multiple_of(j * step, step), step)

        def term(part, whole):
            if split_left:
                return dot(part[:, at], whole, TN)
            return dot(whole[:, at], part[...], TN)

        def of(ref):
            return ref[...] if split_left else ref

        total = term(halves[0], of(wholes[0]))
        total += term(halves[1], of(wholes[1]))
        total += term(halves[4], of(wholes[3]))
        if split_left:
            total += term(halves[2], wholes[2][:half, :])
            total += term(halves[3], wholes[2][half:, :])
        else:
            total += dot(wholes[2][:half, at], halves[2][...], TN)
            total += dot(wholes[2][half:, at], halves[3][...], TN)
        out_ref[at, :] = total.astype(BF16)
        return carry

    lax.fori_loop(0, out_ref.shape[0] // step, one, 0)


def outer(split_left, halves, wholes):
    split_width, whole_width = halves[0].shape[1], wholes[0].shape[1]
    shape = (split_width, whole_width) if split_left else (whole_width, split_width)
    return pl.pallas_call(
        functools.partial(outer_body, split_left),
        out_shape=jax.ShapeDtypeStruct(shape, BF16),
        in_specs=[pl.BlockSpec(memory_space=pltpu.VMEM)] * 9,
        out_specs=pl.BlockSpec(memory_space=pltpu.VMEM),
        compiler_params=VMEM,
        cost_estimate=pl.CostEstimate(
            flops=8 * wholes[0].shape[0] * split_width * whole_width,
            bytes_accessed=4 * 2 * wholes[0].shape[0] * (split_width + whole_width),
            transcendentals=0,
        ),
    )(*halves, *wholes)


def shift(values, by):
    count = lax.axis_size("cross")
    return lax.ppermute(values, "cross", [(i, (i + by) % count) for i in range(count)])


def near(own):
    return own, shift(own, -1), shift(own, 1)


def far(pieces):
    own, after, before = pieces
    half = own.shape[0] // 2
    return own, after, shift(before[:half], 1), shift(after[half:], -1), before


def transpose(parts):
    return parts[0], shift(parts[3], -1), shift(parts[2], 2), shift(parts[1], 1)


def exchange(values, experts):
    blocks = values.reshape(experts, ROWS, values.shape[1])
    return lax.all_to_all(blocks, "expert", split_axis=0, concat_axis=0, tiled=True).reshape(
        values.shape
    )


def shards(tokens, route_ids, route_weight, cotangent, up_weight, down_weight):
    experts = lax.axis_size("expert")
    count, width = tokens.shape
    place = lax.axis_index("cross").astype(jnp.int32).reshape(1)
    ids, weight = route_ids.T, route_weight.T
    cot_slices = transpose(slices(place, ids, weight, cotangent))
    got_grad = exchange(dispatch_grads(cot_slices, experts), experts)
    ups = far(near(up_weight[0]))
    sent_tokens = dispatch_tokens(place, ids, tokens, experts)
    sent_tokens, ups = lax.optimization_barrier((sent_tokens, ups))
    got_tokens = exchange(sent_tokens, experts)
    *grads, b0, b1, b2, b3 = project(got_grad, down_weight[0])
    backs = transpose((b0, b1, b2, b3))
    x0, x1, x2, x3, hidden, hidden_grad, extra = hidden_grads_of(got_tokens, ups, backs)
    ret = input_grads(hidden_grad, extra, ups, experts)
    back = exchange(ret, experts)
    hiddens = far(near(hidden))
    token_slices = transpose((x0, x1, x2, x3))
    hidden_grads = far(near(hidden_grad))
    grad_down = outer(True, hiddens, grads)
    grad_up = outer(False, hidden_grads, token_slices)
    d_tokens, d_route = combine(place, ids, weight, back, count, width)
    return d_tokens, d_route, grad_up[None], grad_down[None]


def solution(mesh):
    rows = P(("expert", "cross"), None)
    ups, downs = P("expert", "cross", None), P("expert", None, "cross")
    return jax.shard_map(
        shards,
        mesh=mesh,
        in_specs=(rows, rows, rows, rows, ups, downs),
        out_specs=(rows, rows, ups, downs),
        check_vma=False,
    )
```

```python
import functools

import jax
import jax.numpy as jnp
from jax import lax
from jax.experimental import pallas as pl
from jax.experimental.pallas import tpu as pltpu
from jax.sharding import PartitionSpec as P

CAP = 6
ROWS = 8
F32 = jnp.float32
BF16 = jnp.bfloat16
VMEM = pltpu.CompilerParams(vmem_limit_bytes=60 * 1024 * 1024)
NT = (((1,), (1,)), ((), ()))
TN = (((0,), (0,)), ((), ()))


def iota(shape, dim):
    return lax.broadcasted_iota(jnp.int32, shape, dim)


def dot(a, b, dims=None):
    if dims is None:
        return jnp.dot(a, b, preferred_element_type=F32)
    return lax.dot_general(a, b, dims, preferred_element_type=F32)


def slots(first, second):
    count = first.shape[1]
    down, across = iota((count, count), 0), iota((count, count), 1)
    eye = down == across
    earlier = (down < across).astype(F32)
    first_col = jnp.sum(jnp.where(eye, first, 0), axis=1, keepdims=True)
    second_col = jnp.sum(jnp.where(eye, second, 0), axis=1, keepdims=True)

    def total(hits):
        return jnp.sum(hits, axis=0, keepdims=True)

    rank_first = total((first_col == first).astype(F32) * earlier)
    rank_second = total((first_col == second).astype(F32)) + total(
        (second_col == second).astype(F32) * earlier
    )
    return (first, rank_first.astype(jnp.int32)), (second, rank_second.astype(jnp.int32))


def row_of(route):
    return route[0] * ROWS + route[1]


def rest_of(route):
    late = (route[1] >= 3).astype(jnp.int32)
    return route[0] * ROWS + CAP + late, route[1] - 3 * late


def chosen(hit_of, routes, shares):
    return sum(
        jnp.where(hit_of(route), share, 0.0) for route, share in zip(routes, shares)
    ).astype(BF16)


def packed_block(down, part, mine, last):
    def hit_of(route):
        row, column = rest_of(route)
        return (down == row) & (column == part)

    main = chosen(lambda route: down == row_of(route), mine[0], mine[1])
    left = jnp.concatenate([main, chosen(hit_of, last[0], last[1])], axis=1)
    return dot(left, jnp.concatenate([mine[2], last[2]], axis=0)).astype(BF16)


def block_at(place_ref, ref, delta):
    block = ref.shape[1] // 4
    start = lax.rem(place_ref[0] + delta, 4) * block
    return ref[:, pl.ds(pl.multiple_of(start, 128), block)]


def token_body(place_ref, ids_ref, values_ref, out_ref):
    count, width = values_ref.shape
    block = width // 4
    down = iota((out_ref.shape[0], count), 0)
    routes = slots(ids_ref[0:1, :], ids_ref[1:2, :])
    shares = (1.0, 1.0)
    last = (routes, shares, block_at(place_ref, values_ref, 3))
    for part in range(3):
        mine = (routes, shares, block_at(place_ref, values_ref, part))
        out_ref[:, part * block : (part + 1) * block] = packed_block(down, part, mine, last)


def dispatch_tokens(place, ids, values, experts):
    count, width = values.shape
    rows_all = experts * ROWS
    packed = 3 * width // 4
    vmem = pl.BlockSpec(memory_space=pltpu.VMEM)
    return pl.pallas_call(
        token_body,
        out_shape=jax.ShapeDtypeStruct((rows_all, packed), BF16),
        in_specs=[pl.BlockSpec(memory_space=pltpu.SMEM), vmem, vmem],
        out_specs=vmem,
        compiler_params=VMEM,
        cost_estimate=pl.CostEstimate(
            flops=4 * rows_all * count * packed,
            bytes_accessed=2 * (count * width + rows_all * packed),
            transcendentals=0,
        ),
    )(place, ids, values)


NOTES = 16


def slice_body(place_ref, ids_ref, weight_ref, values_ref, *out_refs):
    count, width = values_ref.shape
    block = width // 4
    row = iota((NOTES, count), 0)
    notes = jnp.zeros((NOTES, count), F32)
    for k in range(2):
        notes = jnp.where(row == k, ids_ref[k : k + 1, :].astype(F32), notes)
        notes = jnp.where(row == 2 + k, weight_ref[k : k + 1, :].astype(F32), notes)
    for delta, out_ref in enumerate(out_refs):
        out_ref[:count, :] = block_at(place_ref, values_ref, delta)
        out_ref[count:, :] = jnp.zeros((NOTES, block), BF16)
        out_ref[count:, :count] = notes.astype(BF16)


def slices(place, ids, weight, values):
    count, width = values.shape
    vmem = pl.BlockSpec(memory_space=pltpu.VMEM)
    return pl.pallas_call(
        slice_body,
        out_shape=[jax.ShapeDtypeStruct((count + NOTES, width // 4), BF16)] * 4,
        in_specs=[pl.BlockSpec(memory_space=pltpu.SMEM), vmem, vmem, vmem],
        out_specs=[vmem] * 4,
        compiler_params=VMEM,
        cost_estimate=pl.CostEstimate(
            flops=0, bytes_accessed=4 * count * width, transcendentals=0
        ),
    )(place, ids, weight, values)


def grad_body(s0, s1, s2, s3, out_ref):
    count = s0.shape[0] - NOTES
    block = s0.shape[1]
    down = iota((out_ref.shape[0], count), 0)
    groups = []
    for ref in (s0, s1, s2, s3):
        notes = ref[count:, :count].astype(F32)
        first, second = (notes[k : k + 1, :].astype(jnp.int32) for k in range(2))
        groups.append((slots(first, second), (notes[2:3, :], notes[3:4, :]), ref[:count, :]))
    for part in range(3):
        out_ref[:, part * block : (part + 1) * block] = packed_block(
            down, part, groups[part], groups[3]
        )


def dispatch_grads(parts, experts):
    count, block = parts[0].shape
    rows_all = experts * ROWS
    vmem = pl.BlockSpec(memory_space=pltpu.VMEM)
    return pl.pallas_call(
        grad_body,
        out_shape=jax.ShapeDtypeStruct((rows_all, 3 * block), BF16),
        in_specs=[vmem] * 4,
        out_specs=vmem,
        compiler_params=VMEM,
        cost_estimate=pl.CostEstimate(
            flops=12 * rows_all * count * block,
            bytes_accessed=2 * (4 * count + 3 * rows_all) * block,
            transcendentals=0,
        ),
    )(*parts)


def pickers(experts):
    rows, packed = experts * CAP, experts * ROWS
    at, column = iota((rows, packed), 0), iota((rows, packed), 1)
    expert = lax.shift_right_logical(at * 10923, 16)
    slot = at - expert * CAP
    late = (slot >= 3).astype(jnp.int32)
    main = (column == expert * ROWS + slot).astype(BF16)
    rest = [
        ((column == expert * ROWS + CAP + late) & (slot - 3 * late == part)).astype(BF16)
        for part in range(3)
    ]
    return main, rest


def packers(experts):
    rows, packed = experts * CAP, experts * ROWS
    at, column = iota((packed, rows), 1), iota((packed, rows), 0)
    expert = lax.shift_right_logical(at * 10923, 16)
    slot = at - expert * CAP
    late = (slot >= 3).astype(jnp.int32)
    main = (column == expert * ROWS + slot).astype(BF16)
    rest = [
        ((column == expert * ROWS + CAP + late) & (slot - 3 * late == part)).astype(BF16)
        for part in range(3)
    ]
    return main, rest


def group_size(rows_all):
    experts = rows_all // ROWS
    return min(32, experts)


def unpack(packed_ref, whole_refs):
    rows_all, packed = packed_ref.shape
    block = packed // 3
    size = group_size(rows_all)
    main, rest = pickers(size)
    for group in range(rows_all // (size * ROWS)):
        source = slice(group * size * ROWS, (group + 1) * size * ROWS)
        target = slice(group * size * CAP, (group + 1) * size * CAP)
        parts = [packed_ref[source, part * block : (part + 1) * block] for part in range(3)]
        for part in range(3):
            whole_refs[part][target, :] = dot(main, parts[part]).astype(BF16)
        whole_refs[3][target, :] = sum(dot(rest[part], parts[part]) for part in range(3)).astype(
            BF16
        )


def project_body(got_ref, down_ref, g0, g1, g2, g3, b0, b1, b2, b3):
    wholes = (g0, g1, g2, g3)
    unpack(got_ref, wholes)
    hidden_width = down_ref.shape[0]
    step = min(256, hidden_width)
    for j in range(hidden_width // step):
        at = slice(j * step, (j + 1) * step)
        weight = down_ref[at, :]
        for whole, out_ref in zip(wholes, (b0, b1, b2, b3)):
            out_ref[:, at] = dot(whole[...], weight, NT).astype(out_ref.dtype)


def project(got, down):
    rows_all, packed = got.shape
    rows = rows_all // ROWS * CAP
    block, hidden_width = packed // 3, down.shape[0]
    return pl.pallas_call(
        project_body,
        out_shape=[jax.ShapeDtypeStruct((rows, block), BF16)] * 4
        + [jax.ShapeDtypeStruct((rows, hidden_width), F32)]
        + [jax.ShapeDtypeStruct((rows, hidden_width), BF16)] * 3,
        in_specs=[pl.BlockSpec(memory_space=pltpu.VMEM)] * 2,
        out_specs=[pl.BlockSpec(memory_space=pltpu.VMEM)] * 8,
        compiler_params=VMEM,
        cost_estimate=pl.CostEstimate(
            flops=10 * rows * block * hidden_width,
            bytes_accessed=12 * rows * (block + hidden_width),
            transcendentals=0,
        ),
    )(got, down)


def unpack_rows_body(got_ref, x0, x1, x2, x3):
    unpack(got_ref, (x0, x1, x2, x3))


def unpack_rows(got):
    rows_all, packed = got.shape
    size = group_size(rows_all)
    block = packed // 3
    return pl.pallas_call(
        unpack_rows_body,
        grid=(rows_all // (size * ROWS),),
        out_shape=[jax.ShapeDtypeStruct((rows_all // ROWS * CAP, block), BF16)] * 4,
        in_specs=[pl.BlockSpec((size * ROWS, packed), lambda i: (i, 0))],
        out_specs=[pl.BlockSpec((size * CAP, block), lambda i: (i, 0))] * 4,
        compiler_params=VMEM,
        cost_estimate=pl.CostEstimate(
            flops=12 * rows_all * size * CAP * block,
            bytes_accessed=4 * rows_all * packed,
            transcendentals=0,
        ),
    )(got)


def expert_body(
    x0, x1, x2, x3, b0, b1, b2, b3, up0, up1, up2a, up2b, up3,
    hidden_ref, hgrad_ref, ret_ref, w0, w1, w2, w3, p0, p1, p2, p3, sems,
):
    rows, hidden_width = hidden_ref.shape
    block = w0.shape[0]
    half = block // 2
    step = min(256, hidden_width)
    sources = (up0, up1, up2a, up2b, up3, b0, b1, b2, b3)
    places = (w0, w1, w2.at[:half, :], w2.at[half:, :], w3, p0, p1, p2, p3)
    copies = []
    for j in range(hidden_width // step):
        at = slice(j * step, (j + 1) * step)
        copies.append(
            [
                pltpu.make_async_copy(source.at[:, at], target.at[:, at], sems.at[p, j])
                for p, (source, target) in enumerate(zip(sources, places))
            ]
        )
        for copy in copies[-1]:
            copy.start()
    score = jnp.zeros((rows, 1), F32)
    for j, group in enumerate(copies):
        at = slice(j * step, (j + 1) * step)
        for copy in group:
            copy.wait()
        pre_act = dot(x0[...], w0[:, at])
        pre_act += dot(x1[...], w1[:, at])
        pre_act += dot(x2[...], w2[:, at])
        pre_act += dot(x3[...], w3[:, at])
        back = p0[:, at] + p1[:, at].astype(F32) + p2[:, at].astype(F32) + p3[:, at].astype(F32)
        sigmoid_val = jax.nn.sigmoid(pre_act)
        hidden = (pre_act * sigmoid_val).astype(BF16)
        hidden_ref[:, at] = hidden
        slope = sigmoid_val * (1.0 + pre_act * (1.0 - sigmoid_val))
        hgrad_ref[:, at] = (back * slope).astype(BF16)
        score += jnp.sum(hidden.astype(F32) * back, axis=1, keepdims=True)

    size = group_size(ret_ref.shape[0])
    main, rest = packers(size)
    groups = [
        (slice(g * size * CAP, (g + 1) * size * CAP), slice(g * size * ROWS, (g + 1) * size * ROWS))
        for g in range(rows // (size * CAP))
    ]
    whole = hgrad_ref[...]
    chunk = min(256, block)
    for n in range(block // chunk):
        at = slice(n * chunk, (n + 1) * chunk)
        last = dot(whole, w3[at, :], NT).astype(BF16)
        for part, weight in enumerate((w0, w1, w2)):
            here = dot(whole, weight[at, :], NT).astype(BF16)
            start = part * block + n * chunk
            for source, target in groups:
                ret_ref[target, start : start + chunk] = (
                    dot(main, here[source]) + dot(rest[part], last[source])
                ).astype(BF16)
    high = score.astype(BF16)
    low = (score - high.astype(F32)).astype(BF16)
    lane = iota((rows, 128), 1)
    extra = jnp.where(lane == 0, high.astype(F32), jnp.where(lane == 1, low.astype(F32), 0.0))
    extra = extra.astype(BF16)
    for source, target in groups:
        ret_ref[target, 3 * block :] = dot(main, extra[source]).astype(BF16)


def expert(wholes, ups, backs, experts):
    rows, block = wholes[0].shape
    hidden_width = ups[0].shape[1]
    vmem = pl.BlockSpec(memory_space=pltpu.VMEM)
    return pl.pallas_call(
        expert_body,
        out_shape=[jax.ShapeDtypeStruct((rows, hidden_width), BF16)] * 2
        + [jax.ShapeDtypeStruct((experts * ROWS, 3 * block + 128), BF16)],
        in_specs=[vmem] * 4 + [pl.BlockSpec(memory_space=pl.ANY)] * 9,
        out_specs=[vmem] * 3,
        scratch_shapes=[pltpu.VMEM((block, hidden_width), BF16)] * 4
        + [pltpu.VMEM((rows, hidden_width), F32)]
        + [pltpu.VMEM((rows, hidden_width), BF16)] * 3
        + [pltpu.SemaphoreType.DMA((9, hidden_width // min(256, hidden_width)))],
        compiler_params=VMEM,
        cost_estimate=pl.CostEstimate(
            flops=20 * rows * block * hidden_width,
            bytes_accessed=24 * block * hidden_width,
            transcendentals=rows * hidden_width,
        ),
    )(*wholes, *backs, *ups)


def combine_body(place_ref, ids_ref, weight_ref, ret_ref, dtok_ref, droute_ref):
    rows_all = ret_ref.shape[0]
    count, width = dtok_ref.shape
    block = width // 4
    routes = slots(ids_ref[0:1, :], ids_ref[1:2, :])
    eye = iota((count, count), 0) == iota((count, count), 1)

    def col(row):
        return jnp.sum(jnp.where(eye, row, jnp.zeros_like(row)), axis=1, keepdims=True)

    across = iota((count, rows_all), 1)
    hits = [(across == col(row_of(route))).astype(BF16) for route in routes]
    main = hits[0] + hits[1]
    rests = [rest_of(route) for route in routes]
    rest_rows = [col(row) for row, _ in rests]
    rest_parts = [col(part) for _, part in rests]

    def put(delta, values):
        start = lax.rem(place_ref[0] + delta, 4) * block
        dtok_ref[:, pl.ds(pl.multiple_of(start, 128), block)] = values.astype(BF16)

    last = jnp.zeros((count, block), F32)
    for part in range(3):
        got = ret_ref[:, part * block : (part + 1) * block]
        put(part, dot(main, got))
        pick = sum(
            ((across == row) & (column == part)).astype(F32)
            for row, column in zip(rest_rows, rest_parts)
        ).astype(BF16)
        last += dot(pick, got)
    put(3, last)
    extra = ret_ref[:, 3 * block :]
    lane = iota((count, 2), 1)
    out = jnp.zeros((count, 2), F32)
    for k in range(2):
        pair = dot(hits[k], extra)
        value = (pair[:, 0:1] + pair[:, 1:2]) / col(weight_ref[k : k + 1, :].astype(F32))
        out = jnp.where(lane == k, value, out)
    droute_ref[...] = out.astype(BF16)


def combine(place, ids, weight, ret, count, width):
    vmem = pl.BlockSpec(memory_space=pltpu.VMEM)
    return pl.pallas_call(
        combine_body,
        out_shape=[
            jax.ShapeDtypeStruct((count, width), BF16),
            jax.ShapeDtypeStruct((count, 2), BF16),
        ],
        in_specs=[pl.BlockSpec(memory_space=pltpu.SMEM), vmem, vmem, vmem],
        out_specs=[vmem, vmem],
        compiler_params=VMEM,
        cost_estimate=pl.CostEstimate(
            flops=4 * ret.shape[0] * count * width,
            bytes_accessed=2 * (count * width + ret.size),
            transcendentals=0,
        ),
    )(place, ids, weight, ret)


def near_body(l0, l1, l3, r0, r1, r3, out_ref):
    step = min(256, out_ref.shape[0])

    def one(j, carry):
        at = pl.ds(pl.multiple_of(j * step, step), step)
        total = dot(l0[:, at], r0[...], TN)
        total += dot(l1[:, at], r1[...], TN)
        total += dot(l3[:, at], r3[...], TN)
        out_ref[at, :] = total
        return carry

    lax.fori_loop(0, out_ref.shape[0] // step, one, 0)


def outer_near(lefts, rights):
    rows, shape = lefts[0].shape[0], (lefts[0].shape[1], rights[0].shape[1])
    return pl.pallas_call(
        near_body,
        out_shape=jax.ShapeDtypeStruct(shape, F32),
        in_specs=[pl.BlockSpec(memory_space=pltpu.VMEM)] * 6,
        out_specs=pl.BlockSpec(memory_space=pltpu.VMEM),
        compiler_params=VMEM,
        cost_estimate=pl.CostEstimate(
            flops=6 * rows * shape[0] * shape[1],
            bytes_accessed=6 * rows * sum(shape) + 4 * shape[0] * shape[1],
            transcendentals=0,
        ),
    )(*lefts, *rights)


def last_body(left_in_halves, total_ref, whole, first, second, out_ref):
    half = first.shape[0]
    step = min(256, out_ref.shape[0])

    def one(j, carry):
        at = pl.ds(pl.multiple_of(j * step, step), step)
        total = total_ref[at, :]
        if left_in_halves:
            total += dot(first[:, at], whole[:half, :], TN)
            total += dot(second[:, at], whole[half:, :], TN)
        else:
            total += dot(whole[:half, at], first[...], TN)
            total += dot(whole[half:, at], second[...], TN)
        out_ref[at, :] = total.astype(BF16)
        return carry

    lax.fori_loop(0, out_ref.shape[0] // step, one, 0)


def outer_last(left_in_halves, total, whole, first, second):
    return pl.pallas_call(
        functools.partial(last_body, left_in_halves),
        out_shape=jax.ShapeDtypeStruct(total.shape, BF16),
        in_specs=[pl.BlockSpec(memory_space=pltpu.VMEM)] * 4,
        out_specs=pl.BlockSpec(memory_space=pltpu.VMEM),
        compiler_params=VMEM,
        cost_estimate=pl.CostEstimate(
            flops=2 * whole.shape[0] * total.shape[0] * total.shape[1],
            bytes_accessed=6 * total.size + 2 * whole.shape[0] * sum(total.shape),
            transcendentals=0,
        ),
    )(total, whole, first, second)


def shift(values, by):
    count = lax.axis_size("cross")
    return lax.ppermute(values, "cross", [(i, (i + by) % count) for i in range(count)])


def near(own):
    return own, shift(own, -1), shift(own, 1)


def far(pieces):
    own, after, before = pieces
    half = own.shape[0] // 2
    return own, after, shift(before[:half], 1), shift(after[half:], -1), before


def transpose(parts):
    return parts[0], shift(parts[3], -1), shift(parts[2], 2), shift(parts[1], 1)


def exchange(values, experts):
    blocks = values.reshape(experts, ROWS, values.shape[1])
    return lax.all_to_all(blocks, "expert", split_axis=0, concat_axis=0, tiled=True).reshape(
        values.shape
    )


def shards(tokens, route_ids, route_weight, cotangent, up_weight, down_weight):
    experts = lax.axis_size("expert")
    count, width = tokens.shape
    place = lax.axis_index("cross").astype(jnp.int32).reshape(1)
    ids, weight = route_ids.T, route_weight.T
    cot_slices = transpose(slices(place, ids, weight, cotangent))
    got_grad = exchange(dispatch_grads(cot_slices, experts), experts)
    ups_near = near(up_weight[0])
    sent_tokens = dispatch_tokens(place, ids, tokens, experts)
    sent_tokens, ups_near = lax.optimization_barrier((sent_tokens, ups_near))
    ups = far(ups_near)
    got_tokens = exchange(sent_tokens, experts)
    g0, g1, g2, g3, b0, b1, b2, b3 = project(got_grad, down_weight[0])
    backs = transpose((b0, b1, b2, b3))
    got_tokens, backs, ups = lax.optimization_barrier((got_tokens, backs, ups))
    wholes = unpack_rows(got_tokens)
    t1, t3 = shift(wholes[3], -1), shift(wholes[1], 1)
    hidden, hidden_grad, ret = expert(wholes, ups, backs, experts)
    ret, t1, t3 = lax.optimization_barrier((ret, t1, t3))
    back = exchange(ret, experts)
    h0, h1, h2a, h2b, h3 = far(near(hidden))
    d0, d1, d2a, d2b, d3 = far(near(hidden_grad))
    t2 = shift(wholes[2], 2)
    down_near = outer_near((h0, h1, h3), (g0, g1, g3))
    up_near = outer_near((wholes[0], t1, t3), (d0, d1, d3))
    grad_down = outer_last(True, down_near, g2, h2a, h2b)
    back, grad_down, up_near = lax.optimization_barrier((back, grad_down, up_near))
    d_tokens, d_route = combine(place, ids, weight, back, count, width)
    up_near, d_tokens, d_route = lax.optimization_barrier((up_near, d_tokens, d_route))
    grad_up = outer_last(False, up_near, t2, d2a, d2b)
    return d_tokens, d_route, grad_up[None], grad_down[None]


def solution(mesh):
    rows = P(("expert", "cross"), None)
    ups, downs = P("expert", "cross", None), P("expert", None, "cross")
    return jax.shard_map(
        shards,
        mesh=mesh,
        in_specs=(rows, rows, rows, rows, ups, downs),
        out_specs=(rows, rows, ups, downs),
        check_vma=False,
    )
```

```python
import functools

import jax
import jax.numpy as jnp
from jax import lax
from jax.experimental import pallas as pl
from jax.experimental.pallas import tpu as pltpu
from jax.sharding import PartitionSpec as P

CAP = 6
ROWS = 8
F32 = jnp.float32
BF16 = jnp.bfloat16


def vmem(mebibytes):
    return pltpu.CompilerParams(vmem_limit_bytes=mebibytes * 1024 * 1024)


NT = (((1,), (1,)), ((), ()))
TN = (((0,), (0,)), ((), ()))


def iota(shape, dim):
    return lax.broadcasted_iota(jnp.int32, shape, dim)


def dot(a, b, dims=None):
    if dims is None:
        return jnp.dot(a, b, preferred_element_type=F32)
    return lax.dot_general(a, b, dims, preferred_element_type=F32)


def slots(first, second):
    count = first.shape[1]
    down, across = iota((count, count), 0), iota((count, count), 1)
    eye = down == across
    earlier = (down < across).astype(F32)
    first_col = jnp.sum(jnp.where(eye, first, 0), axis=1, keepdims=True)
    second_col = jnp.sum(jnp.where(eye, second, 0), axis=1, keepdims=True)

    def total(hits):
        return jnp.sum(hits, axis=0, keepdims=True)

    rank_first = total((first_col == first).astype(F32) * earlier)
    rank_second = total((first_col == second).astype(F32)) + total(
        (second_col == second).astype(F32) * earlier
    )
    return (first, rank_first.astype(jnp.int32)), (second, rank_second.astype(jnp.int32))


def row_of(route):
    return route[0] * ROWS + route[1]


def rest_of(route):
    late = (route[1] >= 3).astype(jnp.int32)
    return route[0] * ROWS + CAP + late, route[1] - 3 * late


def chosen(hit_of, routes, shares):
    return sum(
        jnp.where(hit_of(route), share, 0.0) for route, share in zip(routes, shares)
    ).astype(BF16)


def packed_block(down, part, mine, last):
    def hit_of(route):
        row, column = rest_of(route)
        return (down == row) & (column == part)

    main = chosen(lambda route: down == row_of(route), mine[0], mine[1])
    left = jnp.concatenate([main, chosen(hit_of, last[0], last[1])], axis=1)
    return dot(left, jnp.concatenate([mine[2], last[2]], axis=0)).astype(BF16)


def block_at(place_ref, ref, delta):
    block = ref.shape[1] // 4
    start = lax.rem(place_ref[0] + delta, 4) * block
    return ref[:, pl.ds(pl.multiple_of(start, 128), block)]


def token_body(place_ref, ids_ref, values_ref, out_ref):
    count, width = values_ref.shape
    block = width // 4
    down = iota((out_ref.shape[0], count), 0)
    routes = slots(ids_ref[0:1, :], ids_ref[1:2, :])
    shares = (1.0, 1.0)
    last = (routes, shares, block_at(place_ref, values_ref, 3))
    for part in range(3):
        mine = (routes, shares, block_at(place_ref, values_ref, part))
        out_ref[:, part * block : (part + 1) * block] = packed_block(down, part, mine, last)


def dispatch_tokens(place, ids, values, experts):
    count, width = values.shape
    rows_all = experts * ROWS
    packed = 3 * width // 4
    spec = pl.BlockSpec(memory_space=pltpu.VMEM)
    return pl.pallas_call(
        token_body,
        out_shape=jax.ShapeDtypeStruct((rows_all, packed), BF16),
        in_specs=[pl.BlockSpec(memory_space=pltpu.SMEM), spec, spec],
        out_specs=spec,
        compiler_params=vmem(60),
        cost_estimate=pl.CostEstimate(
            flops=4 * rows_all * count * packed,
            bytes_accessed=2 * (count * width + rows_all * packed),
            transcendentals=0,
        ),
    )(place, ids, values)


NOTES = 16


def slice_body(place_ref, ids_ref, weight_ref, values_ref, *out_refs):
    count, width = values_ref.shape
    block = width // 4
    row = iota((NOTES, count), 0)
    notes = jnp.zeros((NOTES, count), F32)
    for k in range(2):
        notes = jnp.where(row == k, ids_ref[k : k + 1, :].astype(F32), notes)
        notes = jnp.where(row == 2 + k, weight_ref[k : k + 1, :].astype(F32), notes)
    for delta, out_ref in enumerate(out_refs):
        out_ref[:count, :] = block_at(place_ref, values_ref, delta)
        out_ref[count:, :] = jnp.zeros((NOTES, block), BF16)
        out_ref[count:, :count] = notes.astype(BF16)


def slices(place, ids, weight, values):
    count, width = values.shape
    spec = pl.BlockSpec(memory_space=pltpu.VMEM)
    return pl.pallas_call(
        slice_body,
        out_shape=[jax.ShapeDtypeStruct((count + NOTES, width // 4), BF16)] * 4,
        in_specs=[pl.BlockSpec(memory_space=pltpu.SMEM), spec, spec, spec],
        out_specs=[spec] * 4,
        compiler_params=vmem(60),
        cost_estimate=pl.CostEstimate(
            flops=0, bytes_accessed=4 * count * width, transcendentals=0
        ),
    )(place, ids, weight, values)


def grad_body(s0, s1, s2, s3, out_ref):
    count = s0.shape[0] - NOTES
    block = s0.shape[1]
    down = iota((out_ref.shape[0], count), 0)
    groups = []
    for ref in (s0, s1, s2, s3):
        notes = ref[count:, :count].astype(F32)
        first, second = (notes[k : k + 1, :].astype(jnp.int32) for k in range(2))
        groups.append((slots(first, second), (notes[2:3, :], notes[3:4, :]), ref[:count, :]))
    for part in range(3):
        out_ref[:, part * block : (part + 1) * block] = packed_block(
            down, part, groups[part], groups[3]
        )


def dispatch_grads(parts, experts):
    count, block = parts[0].shape
    rows_all = experts * ROWS
    spec = pl.BlockSpec(memory_space=pltpu.VMEM)
    return pl.pallas_call(
        grad_body,
        out_shape=jax.ShapeDtypeStruct((rows_all, 3 * block), BF16),
        in_specs=[spec] * 4,
        out_specs=spec,
        compiler_params=vmem(60),
        cost_estimate=pl.CostEstimate(
            flops=12 * rows_all * count * block,
            bytes_accessed=2 * (4 * count + 3 * rows_all) * block,
            transcendentals=0,
        ),
    )(*parts)


def pickers(experts):
    rows, packed = experts * CAP, experts * ROWS
    at, column = iota((rows, packed), 0), iota((rows, packed), 1)
    expert = lax.shift_right_logical(at * 10923, 16)
    slot = at - expert * CAP
    late = (slot >= 3).astype(jnp.int32)
    main = (column == expert * ROWS + slot).astype(BF16)
    rest = [
        ((column == expert * ROWS + CAP + late) & (slot - 3 * late == part)).astype(BF16)
        for part in range(3)
    ]
    return main, rest


def packers(experts):
    rows, packed = experts * CAP, experts * ROWS
    at, column = iota((packed, rows), 1), iota((packed, rows), 0)
    expert = lax.shift_right_logical(at * 10923, 16)
    slot = at - expert * CAP
    late = (slot >= 3).astype(jnp.int32)
    main = (column == expert * ROWS + slot).astype(BF16)
    rest = [
        ((column == expert * ROWS + CAP + late) & (slot - 3 * late == part)).astype(BF16)
        for part in range(3)
    ]
    return main, rest


def group_size(rows_all):
    experts = rows_all // ROWS
    return min(32, experts)


def unpack(packed_ref, whole_refs):
    rows_all, packed = packed_ref.shape
    block = packed // 3
    size = group_size(rows_all)
    main, rest = pickers(size)
    for group in range(rows_all // (size * ROWS)):
        source = slice(group * size * ROWS, (group + 1) * size * ROWS)
        target = slice(group * size * CAP, (group + 1) * size * CAP)
        parts = [packed_ref[source, part * block : (part + 1) * block] for part in range(3)]
        for part in range(3):
            whole_refs[part][target, :] = dot(main, parts[part]).astype(BF16)
        whole_refs[3][target, :] = sum(dot(rest[part], parts[part]) for part in range(3)).astype(
            BF16
        )


def project_body(got_ref, down_ref, g0, g1, g2, g3, b0, b1, b2, b3):
    wholes = (g0, g1, g2, g3)
    unpack(got_ref, wholes)
    hidden_width = down_ref.shape[0]
    step = min(256, hidden_width)
    for j in range(hidden_width // step):
        at = slice(j * step, (j + 1) * step)
        weight = down_ref[at, :]
        for whole, out_ref in zip(wholes, (b0, b1, b2, b3)):
            out_ref[:, at] = dot(whole[...], weight, NT).astype(out_ref.dtype)


def project(got, down):
    rows_all, packed = got.shape
    rows = rows_all // ROWS * CAP
    block, hidden_width = packed // 3, down.shape[0]
    return pl.pallas_call(
        project_body,
        out_shape=[jax.ShapeDtypeStruct((rows, block), BF16)] * 4
        + [jax.ShapeDtypeStruct((rows, hidden_width), F32)]
        + [jax.ShapeDtypeStruct((rows, hidden_width), BF16)] * 3,
        in_specs=[pl.BlockSpec(memory_space=pltpu.VMEM)] * 2,
        out_specs=[pl.BlockSpec(memory_space=pltpu.VMEM)] * 8,
        compiler_params=vmem(60),
        cost_estimate=pl.CostEstimate(
            flops=10 * rows * block * hidden_width,
            bytes_accessed=12 * rows * (block + hidden_width),
            transcendentals=0,
        ),
    )(got, down)


def unpack_rows_body(got_ref, x0, x1, x2, x3):
    unpack(got_ref, (x0, x1, x2, x3))


def unpack_rows(got):
    rows_all, packed = got.shape
    size = group_size(rows_all)
    block = packed // 3
    return pl.pallas_call(
        unpack_rows_body,
        grid=(rows_all // (size * ROWS),),
        out_shape=[jax.ShapeDtypeStruct((rows_all // ROWS * CAP, block), BF16)] * 4,
        in_specs=[pl.BlockSpec((size * ROWS, packed), lambda i: (i, 0))],
        out_specs=[pl.BlockSpec((size * CAP, block), lambda i: (i, 0))] * 4,
        compiler_params=vmem(12),
        cost_estimate=pl.CostEstimate(
            flops=12 * rows_all * size * CAP * block,
            bytes_accessed=4 * rows_all * packed,
            transcendentals=0,
        ),
    )(got)


def expert_body(
    x0, x1, x2, x3, up0, up1, up2a, up2b, up3, b0, b1, b2, b3,
    hidden_out, hgrad_out, ret_out,
    w0, w1, w2, w3, p0, p1, p2, p3, hidden_ref, hgrad_ref, ret_ref, in_sems, row_sems, ret_sems,
):
    rows, hidden_width = hidden_ref.shape
    block = w0.shape[0]
    half = block // 2
    step = min(256, hidden_width)
    steps = hidden_width // step
    sources = (up0, up1, up2a, up2b, up3, b0, b1, b2, b3)
    places = (w0, w1, w2.at[:half, :], w2.at[half:, :], w3, p0, p1, p2, p3)

    def fetch(j):
        at = slice(j * step, (j + 1) * step)
        group = [
            pltpu.make_async_copy(source.at[:, at], place.at[:, at], in_sems.at[p, j])
            for p, (source, place) in enumerate(zip(sources, places))
        ]
        for copy in group:
            copy.start()
        return group

    fetched = [fetch(0)]
    leaving = []
    score = jnp.zeros((rows, 1), F32)
    for j in range(steps):
        at = slice(j * step, (j + 1) * step)
        if j + 1 < steps:
            fetched.append(fetch(j + 1))
        for copy in fetched[j]:
            copy.wait()
        pre_act = dot(x0[...], w0[:, at])
        pre_act += dot(x1[...], w1[:, at])
        pre_act += dot(x2[...], w2[:, at])
        pre_act += dot(x3[...], w3[:, at])
        back = p0[:, at] + p1[:, at].astype(F32) + p2[:, at].astype(F32) + p3[:, at].astype(F32)
        sigmoid_val = jax.nn.sigmoid(pre_act)
        hidden = (pre_act * sigmoid_val).astype(BF16)
        hidden_ref[:, at] = hidden
        slope = sigmoid_val * (1.0 + pre_act * (1.0 - sigmoid_val))
        hgrad_ref[:, at] = (back * slope).astype(BF16)
        score += jnp.sum(hidden.astype(F32) * back, axis=1, keepdims=True)
        for k, (ref, out) in enumerate(((hidden_ref, hidden_out), (hgrad_ref, hgrad_out))):
            leaving.append(pltpu.make_async_copy(ref.at[:, at], out.at[:, at], row_sems.at[k, j]))
            leaving[-1].start()

    size = group_size(ret_ref.shape[0])
    main, rest = packers(size)
    groups = [
        (slice(g * size * CAP, (g + 1) * size * CAP), slice(g * size * ROWS, (g + 1) * size * ROWS))
        for g in range(rows // (size * CAP))
    ]
    high = score.astype(BF16)
    low = (score - high.astype(F32)).astype(BF16)
    lane = iota((rows, 128), 1)
    extra = jnp.where(lane == 0, high.astype(F32), jnp.where(lane == 1, low.astype(F32), 0.0))
    extra = extra.astype(BF16)
    for source, target in groups:
        ret_ref[target, 3 * block :] = dot(main, extra[source]).astype(BF16)

    def leave(start, width, at):
        copy = pltpu.make_async_copy(
            ret_ref.at[:, start : start + width], ret_out.at[:, start : start + width], ret_sems.at[at]
        )
        copy.start()
        leaving.append(copy)

    leave(3 * block, 128, 0)
    whole = hgrad_ref[...]
    chunk = min(256, block)
    for n in range(block // chunk):
        at = slice(n * chunk, (n + 1) * chunk)
        last = dot(whole, w3[at, :], NT).astype(BF16)
        for part, weight in enumerate((w0, w1, w2)):
            here = dot(whole, weight[at, :], NT).astype(BF16)
            start = part * block + n * chunk
            for source, target in groups:
                ret_ref[target, start : start + chunk] = (
                    dot(main, here[source]) + dot(rest[part], last[source])
                ).astype(BF16)
            leave(start, chunk, 1 + 3 * n + part)
    for copy in leaving:
        copy.wait()


def expert(wholes, ups, backs, experts):
    rows, block = wholes[0].shape
    hidden_width = ups[0].shape[1]
    packed = (experts * ROWS, 3 * block + 128)
    steps, chunks = hidden_width // min(256, hidden_width), block // min(256, block)
    spec = pl.BlockSpec(memory_space=pltpu.VMEM)
    anywhere = pl.BlockSpec(memory_space=pl.ANY)
    return pl.pallas_call(
        expert_body,
        out_shape=[jax.ShapeDtypeStruct((rows, hidden_width), BF16)] * 2
        + [jax.ShapeDtypeStruct(packed, BF16)],
        in_specs=[spec] * 4 + [anywhere] * 9,
        out_specs=[anywhere] * 3,
        scratch_shapes=[pltpu.VMEM((block, hidden_width), BF16)] * 4
        + [pltpu.VMEM((rows, hidden_width), F32)]
        + [pltpu.VMEM((rows, hidden_width), BF16)] * 5
        + [pltpu.VMEM(packed, BF16)]
        + [
            pltpu.SemaphoreType.DMA((9, steps)),
            pltpu.SemaphoreType.DMA((2, steps)),
            pltpu.SemaphoreType.DMA((1 + 3 * chunks,)),
        ],
        compiler_params=vmem(60),
        cost_estimate=pl.CostEstimate(
            flops=20 * rows * block * hidden_width,
            bytes_accessed=24 * block * hidden_width,
            transcendentals=rows * hidden_width,
        ),
    )(*wholes, *ups, *backs)


def combine_body(place_ref, ids_ref, weight_ref, ret_ref, dtok_ref, droute_ref):
    rows_all = ret_ref.shape[0]
    count, width = dtok_ref.shape
    block = width // 4
    routes = slots(ids_ref[0:1, :], ids_ref[1:2, :])
    eye = iota((count, count), 0) == iota((count, count), 1)

    def col(row):
        return jnp.sum(jnp.where(eye, row, jnp.zeros_like(row)), axis=1, keepdims=True)

    across = iota((count, rows_all), 1)
    hits = [(across == col(row_of(route))).astype(BF16) for route in routes]
    main = hits[0] + hits[1]
    rests = [rest_of(route) for route in routes]
    rest_rows = [col(row) for row, _ in rests]
    rest_parts = [col(part) for _, part in rests]

    def put(delta, values):
        start = lax.rem(place_ref[0] + delta, 4) * block
        dtok_ref[:, pl.ds(pl.multiple_of(start, 128), block)] = values.astype(BF16)

    last = jnp.zeros((count, block), F32)
    for part in range(3):
        got = ret_ref[:, part * block : (part + 1) * block]
        put(part, dot(main, got))
        pick = sum(
            ((across == row) & (column == part)).astype(F32)
            for row, column in zip(rest_rows, rest_parts)
        ).astype(BF16)
        last += dot(pick, got)
    put(3, last)
    extra = ret_ref[:, 3 * block :]
    lane = iota((count, 2), 1)
    out = jnp.zeros((count, 2), F32)
    for k in range(2):
        pair = dot(hits[k], extra)
        value = (pair[:, 0:1] + pair[:, 1:2]) / col(weight_ref[k : k + 1, :].astype(F32))
        out = jnp.where(lane == k, value, out)
    droute_ref[...] = out.astype(BF16)


def combine(place, ids, weight, ret, count, width):
    spec = pl.BlockSpec(memory_space=pltpu.VMEM)
    return pl.pallas_call(
        combine_body,
        out_shape=[
            jax.ShapeDtypeStruct((count, width), BF16),
            jax.ShapeDtypeStruct((count, 2), BF16),
        ],
        in_specs=[pl.BlockSpec(memory_space=pltpu.SMEM), spec, spec, spec],
        out_specs=[spec, spec],
        compiler_params=vmem(20),
        cost_estimate=pl.CostEstimate(
            flops=4 * ret.shape[0] * count * width,
            bytes_accessed=2 * (count * width + ret.size),
            transcendentals=0,
        ),
    )(place, ids, weight, ret)


def near_body(l0, l1, l3, r0, r1, r3, out_ref):
    step = min(256, out_ref.shape[0])

    def one(j, carry):
        at = pl.ds(pl.multiple_of(j * step, step), step)
        total = dot(l0[:, at], r0[...], TN)
        total += dot(l1[:, at], r1[...], TN)
        total += dot(l3[:, at], r3[...], TN)
        out_ref[at, :] = total
        return carry

    lax.fori_loop(0, out_ref.shape[0] // step, one, 0)


def outer_near(lefts, rights):
    rows, shape = lefts[0].shape[0], (lefts[0].shape[1], rights[0].shape[1])
    return pl.pallas_call(
        near_body,
        out_shape=jax.ShapeDtypeStruct(shape, F32),
        in_specs=[pl.BlockSpec(memory_space=pltpu.VMEM)] * 6,
        out_specs=pl.BlockSpec(memory_space=pltpu.VMEM),
        compiler_params=vmem(16),
        cost_estimate=pl.CostEstimate(
            flops=6 * rows * shape[0] * shape[1],
            bytes_accessed=6 * rows * sum(shape) + 4 * shape[0] * shape[1],
            transcendentals=0,
        ),
    )(*lefts, *rights)


def last_body(left_in_halves, total_ref, whole, first, second, out_ref):
    half = first.shape[0]
    step = min(256, out_ref.shape[0])

    def one(j, carry):
        at = pl.ds(pl.multiple_of(j * step, step), step)
        total = total_ref[at, :]
        if left_in_halves:
            total += dot(first[:, at], whole[:half, :], TN)
            total += dot(second[:, at], whole[half:, :], TN)
        else:
            total += dot(whole[:half, at], first[...], TN)
            total += dot(whole[half:, at], second[...], TN)
        out_ref[at, :] = total.astype(BF16)
        return carry

    lax.fori_loop(0, out_ref.shape[0] // step, one, 0)


def outer_last(left_in_halves, total, whole, first, second):
    return pl.pallas_call(
        functools.partial(last_body, left_in_halves),
        out_shape=jax.ShapeDtypeStruct(total.shape, BF16),
        in_specs=[pl.BlockSpec(memory_space=pltpu.VMEM)] * 4,
        out_specs=pl.BlockSpec(memory_space=pltpu.VMEM),
        compiler_params=vmem(16),
        cost_estimate=pl.CostEstimate(
            flops=2 * whole.shape[0] * total.shape[0] * total.shape[1],
            bytes_accessed=6 * total.size + 2 * whole.shape[0] * sum(total.shape),
            transcendentals=0,
        ),
    )(total, whole, first, second)


def shift(values, by):
    count = lax.axis_size("cross")
    return lax.ppermute(values, "cross", [(i, (i + by) % count) for i in range(count)])


def near(own):
    return own, shift(own, -1), shift(own, 1)


def far(pieces):
    own, after, before = pieces
    half = own.shape[0] // 2
    return own, after, shift(before[:half], 1), shift(after[half:], -1), before


def transpose(parts):
    return parts[0], shift(parts[3], -1), shift(parts[2], 2), shift(parts[1], 1)


def exchange(values, experts):
    blocks = values.reshape(experts, ROWS, values.shape[1])
    return lax.all_to_all(blocks, "expert", split_axis=0, concat_axis=0, tiled=True).reshape(
        values.shape
    )


def shards(tokens, route_ids, route_weight, cotangent, up_weight, down_weight):
    experts = lax.axis_size("expert")
    count, width = tokens.shape
    place = lax.axis_index("cross").astype(jnp.int32).reshape(1)
    ids, weight = route_ids.T, route_weight.T
    cot_slices = transpose(slices(place, ids, weight, cotangent))
    got_grad = exchange(dispatch_grads(cot_slices, experts), experts)
    ups_near = near(up_weight[0])
    sent_tokens = dispatch_tokens(place, ids, tokens, experts)
    sent_tokens, ups_near = lax.optimization_barrier((sent_tokens, ups_near))
    ups = far(ups_near)
    got_tokens = exchange(sent_tokens, experts)
    g0, g1, g2, g3, b0, b1, b2, b3 = project(got_grad, down_weight[0])
    backs = transpose((b0, b1, b2, b3))
    got_tokens, backs, ups = lax.optimization_barrier((got_tokens, backs, ups))
    wholes = unpack_rows(got_tokens)
    t1, t3 = shift(wholes[3], -1), shift(wholes[1], 1)
    hidden, hidden_grad, ret = expert(wholes, ups, backs, experts)
    ret, t1, t3 = lax.optimization_barrier((ret, t1, t3))
    back = exchange(ret, experts)
    h0, h1, h2a, h2b, h3 = far(near(hidden))
    down_near = outer_near((h0, h1, h3), (g0, g1, g3))
    t2 = shift(wholes[2], 2)
    grads_near, down_near = lax.optimization_barrier((near(hidden_grad), down_near))
    d0, d1, d2a, d2b, d3 = far(grads_near)
    up_near = outer_near((wholes[0], t1, t3), (d0, d1, d3))
    grad_down = outer_last(True, down_near, g2, h2a, h2b)
    back, grad_down, up_near = lax.optimization_barrier((back, grad_down, up_near))
    d_tokens, d_route = combine(place, ids, weight, back, count, width)
    up_near, d_tokens, d_route = lax.optimization_barrier((up_near, d_tokens, d_route))
    grad_up = outer_last(False, up_near, t2, d2a, d2b)
    return d_tokens, d_route, grad_up[None], grad_down[None]


def solution(mesh):
    rows = P(("expert", "cross"), None)
    ups, downs = P("expert", "cross", None), P("expert", None, "cross")
    return jax.shard_map(
        shards,
        mesh=mesh,
        in_specs=(rows, rows, rows, rows, ups, downs),
        out_specs=(rows, rows, ups, downs),
        check_vma=False,
    )
```

```python
import functools

import jax
import jax.numpy as jnp
from jax import lax
from jax.experimental import pallas as pl
from jax.experimental.pallas import tpu as pltpu
from jax.sharding import PartitionSpec as P

CAP = 6
ROWS = 8
F32 = jnp.float32
BF16 = jnp.bfloat16


def vmem(mebibytes):
    return pltpu.CompilerParams(vmem_limit_bytes=mebibytes * 1024 * 1024)


NT = (((1,), (1,)), ((), ()))
TN = (((0,), (0,)), ((), ()))


def iota(shape, dim):
    return lax.broadcasted_iota(jnp.int32, shape, dim)


def dot(a, b, dims=None):
    if dims is None:
        return jnp.dot(a, b, preferred_element_type=F32)
    return lax.dot_general(a, b, dims, preferred_element_type=F32)


def slots(first, second):
    count = first.shape[1]
    down, across = iota((count, count), 0), iota((count, count), 1)
    eye = down == across
    earlier = (down < across).astype(F32)
    first_col = jnp.sum(jnp.where(eye, first, 0), axis=1, keepdims=True)
    second_col = jnp.sum(jnp.where(eye, second, 0), axis=1, keepdims=True)

    def total(hits):
        return jnp.sum(hits, axis=0, keepdims=True)

    rank_first = total((first_col == first).astype(F32) * earlier)
    rank_second = total((first_col == second).astype(F32)) + total(
        (second_col == second).astype(F32) * earlier
    )
    return (first, rank_first.astype(jnp.int32)), (second, rank_second.astype(jnp.int32))


def row_of(route):
    return route[0] * ROWS + route[1]


def rest_of(route):
    late = (route[1] >= 3).astype(jnp.int32)
    return route[0] * ROWS + CAP + late, route[1] - 3 * late


def chosen(hit_of, routes, shares):
    return sum(
        jnp.where(hit_of(route), share, 0.0) for route, share in zip(routes, shares)
    ).astype(BF16)


def packed_block(down, part, mine, last):
    def hit_of(route):
        row, column = rest_of(route)
        return (down == row) & (column == part)

    main = chosen(lambda route: down == row_of(route), mine[0], mine[1])
    left = jnp.concatenate([main, chosen(hit_of, last[0], last[1])], axis=1)
    return dot(left, jnp.concatenate([mine[2], last[2]], axis=0)).astype(BF16)


def block_at(place_ref, ref, delta):
    block = ref.shape[1] // 4
    start = lax.rem(place_ref[0] + delta, 4) * block
    return ref[:, pl.ds(pl.multiple_of(start, 128), block)]


def token_body(place_ref, ids_ref, values_ref, out_ref):
    count, width = values_ref.shape
    block = width // 4
    down = iota((out_ref.shape[0], count), 0)
    routes = slots(ids_ref[0:1, :], ids_ref[1:2, :])
    shares = (1.0, 1.0)
    last = (routes, shares, block_at(place_ref, values_ref, 3))
    for part in range(3):
        mine = (routes, shares, block_at(place_ref, values_ref, part))
        out_ref[:, part * block : (part + 1) * block] = packed_block(down, part, mine, last)


def dispatch_tokens(place, ids, values, experts):
    count, width = values.shape
    rows_all = experts * ROWS
    packed = 3 * width // 4
    spec = pl.BlockSpec(memory_space=pltpu.VMEM)
    return pl.pallas_call(
        token_body,
        out_shape=jax.ShapeDtypeStruct((rows_all, packed), BF16),
        in_specs=[pl.BlockSpec(memory_space=pltpu.SMEM), spec, spec],
        out_specs=spec,
        compiler_params=vmem(60),
        cost_estimate=pl.CostEstimate(
            flops=4 * rows_all * count * packed,
            bytes_accessed=2 * (count * width + rows_all * packed),
            transcendentals=0,
        ),
    )(place, ids, values)


NOTES = 16


def slice_body(place_ref, ids_ref, weight_ref, values_ref, *out_refs):
    count, width = values_ref.shape
    block = width // 4
    row = iota((NOTES, count), 0)
    notes = jnp.zeros((NOTES, count), F32)
    for k in range(2):
        notes = jnp.where(row == k, ids_ref[k : k + 1, :].astype(F32), notes)
        notes = jnp.where(row == 2 + k, weight_ref[k : k + 1, :].astype(F32), notes)
    for delta, out_ref in enumerate(out_refs):
        out_ref[:count, :] = block_at(place_ref, values_ref, delta)
        out_ref[count:, :] = jnp.zeros((NOTES, block), BF16)
        out_ref[count:, :count] = notes.astype(BF16)


def slices(place, ids, weight, values):
    count, width = values.shape
    spec = pl.BlockSpec(memory_space=pltpu.VMEM)
    return pl.pallas_call(
        slice_body,
        out_shape=[jax.ShapeDtypeStruct((count + NOTES, width // 4), BF16)] * 4,
        in_specs=[pl.BlockSpec(memory_space=pltpu.SMEM), spec, spec, spec],
        out_specs=[spec] * 4,
        compiler_params=vmem(12),
        cost_estimate=pl.CostEstimate(
            flops=0, bytes_accessed=4 * count * width, transcendentals=0
        ),
    )(place, ids, weight, values)


def grad_body(s0, s1, s2, s3, out_ref):
    count = s0.shape[0] - NOTES
    block = s0.shape[1]
    down = iota((out_ref.shape[0], count), 0)
    groups = []
    for ref in (s0, s1, s2, s3):
        notes = ref[count:, :count].astype(F32)
        first, second = (notes[k : k + 1, :].astype(jnp.int32) for k in range(2))
        groups.append((slots(first, second), (notes[2:3, :], notes[3:4, :]), ref[:count, :]))
    for part in range(3):
        out_ref[:, part * block : (part + 1) * block] = packed_block(
            down, part, groups[part], groups[3]
        )


def dispatch_grads(parts, experts):
    count, block = parts[0].shape
    rows_all = experts * ROWS
    spec = pl.BlockSpec(memory_space=pltpu.VMEM)
    return pl.pallas_call(
        grad_body,
        out_shape=jax.ShapeDtypeStruct((rows_all, 3 * block), BF16),
        in_specs=[spec] * 4,
        out_specs=spec,
        compiler_params=vmem(16),
        cost_estimate=pl.CostEstimate(
            flops=12 * rows_all * count * block,
            bytes_accessed=2 * (4 * count + 3 * rows_all) * block,
            transcendentals=0,
        ),
    )(*parts)


def pickers(experts):
    rows, packed = experts * CAP, experts * ROWS
    at, column = iota((rows, packed), 0), iota((rows, packed), 1)
    expert = lax.shift_right_logical(at * 10923, 16)
    slot = at - expert * CAP
    late = (slot >= 3).astype(jnp.int32)
    main = (column == expert * ROWS + slot).astype(BF16)
    rest = [
        ((column == expert * ROWS + CAP + late) & (slot - 3 * late == part)).astype(BF16)
        for part in range(3)
    ]
    return main, rest


def packers(experts):
    rows, packed = experts * CAP, experts * ROWS
    at, column = iota((packed, rows), 1), iota((packed, rows), 0)
    expert = lax.shift_right_logical(at * 10923, 16)
    slot = at - expert * CAP
    late = (slot >= 3).astype(jnp.int32)
    main = (column == expert * ROWS + slot).astype(BF16)
    rest = [
        ((column == expert * ROWS + CAP + late) & (slot - 3 * late == part)).astype(BF16)
        for part in range(3)
    ]
    return main, rest


def group_size(rows_all):
    experts = rows_all // ROWS
    return min(32, experts)


def unpack(packed_ref, whole_refs):
    rows_all, packed = packed_ref.shape
    block = packed // 3
    size = group_size(rows_all)
    main, rest = pickers(size)
    for group in range(rows_all // (size * ROWS)):
        source = slice(group * size * ROWS, (group + 1) * size * ROWS)
        target = slice(group * size * CAP, (group + 1) * size * CAP)
        parts = [packed_ref[source, part * block : (part + 1) * block] for part in range(3)]
        for part in range(3):
            whole_refs[part][target, :] = dot(main, parts[part]).astype(BF16)
        whole_refs[3][target, :] = sum(dot(rest[part], parts[part]) for part in range(3)).astype(
            BF16
        )


def project_body(got_ref, down_ref, g0, g1, g2, g3, b0, b1, b2, b3):
    wholes = (g0, g1, g2, g3)
    unpack(got_ref, wholes)
    hidden_width = down_ref.shape[0]
    step = min(256, hidden_width)
    for j in range(hidden_width // step):
        at = slice(j * step, (j + 1) * step)
        weight = down_ref[at, :]
        for whole, out_ref in zip(wholes, (b0, b1, b2, b3)):
            out_ref[:, at] = dot(whole[...], weight, NT).astype(out_ref.dtype)


def project(got, down):
    rows_all, packed = got.shape
    rows = rows_all // ROWS * CAP
    block, hidden_width = packed // 3, down.shape[0]
    return pl.pallas_call(
        project_body,
        out_shape=[jax.ShapeDtypeStruct((rows, block), BF16)] * 4
        + [jax.ShapeDtypeStruct((rows, hidden_width), F32)]
        + [jax.ShapeDtypeStruct((rows, hidden_width), BF16)] * 3,
        in_specs=[pl.BlockSpec(memory_space=pltpu.VMEM)] * 2,
        out_specs=[pl.BlockSpec(memory_space=pltpu.VMEM)] * 8,
        compiler_params=vmem(60),
        cost_estimate=pl.CostEstimate(
            flops=10 * rows * block * hidden_width,
            bytes_accessed=12 * rows * (block + hidden_width),
            transcendentals=0,
        ),
    )(got, down)


def unpack_rows_body(got_ref, x0, x1, x2, x3):
    unpack(got_ref, (x0, x1, x2, x3))


def unpack_rows(got):
    rows_all, packed = got.shape
    size = group_size(rows_all)
    block = packed // 3
    return pl.pallas_call(
        unpack_rows_body,
        grid=(rows_all // (size * ROWS),),
        out_shape=[jax.ShapeDtypeStruct((rows_all // ROWS * CAP, block), BF16)] * 4,
        in_specs=[pl.BlockSpec((size * ROWS, packed), lambda i: (i, 0))],
        out_specs=[pl.BlockSpec((size * CAP, block), lambda i: (i, 0))] * 4,
        compiler_params=vmem(12),
        cost_estimate=pl.CostEstimate(
            flops=12 * rows_all * size * CAP * block,
            bytes_accessed=4 * rows_all * packed,
            transcendentals=0,
        ),
    )(got)


def expert_body(
    x0, x1, x2, x3, up0, up1, up2a, up2b, up3, b0, b1, b2, b3,
    hidden_out, hgrad_out, ret_out,
    w0, w1, w2, w3, p0, p1, p2, p3, hidden_ref, hgrad_ref, ret_ref, in_sems, row_sems, ret_sems,
):
    rows, hidden_width = hidden_ref.shape
    block = w0.shape[0]
    half = block // 2
    step = min(512, hidden_width)
    steps = hidden_width // step
    sources = (up0, up1, up2a, up2b, up3, b0, b1, b2, b3)
    places = (w0, w1, w2.at[:half, :], w2.at[half:, :], w3, p0, p1, p2, p3)

    def fetch(j):
        at = slice(j * step, (j + 1) * step)
        group = [
            pltpu.make_async_copy(source.at[:, at], place.at[:, at], in_sems.at[p, j])
            for p, (source, place) in enumerate(zip(sources, places))
        ]
        for copy in group:
            copy.start()
        return group

    fetched = [fetch(0)]
    leaving = []
    score = jnp.zeros((rows, 1), F32)
    for j in range(steps):
        at = slice(j * step, (j + 1) * step)
        if j + 1 < steps:
            fetched.append(fetch(j + 1))
        for copy in fetched[j]:
            copy.wait()
        pre_act = dot(x0[...], w0[:, at])
        pre_act += dot(x1[...], w1[:, at])
        pre_act += dot(x2[...], w2[:, at])
        pre_act += dot(x3[...], w3[:, at])
        back = p0[:, at] + p1[:, at].astype(F32) + p2[:, at].astype(F32) + p3[:, at].astype(F32)
        sigmoid_val = jax.nn.sigmoid(pre_act)
        hidden = (pre_act * sigmoid_val).astype(BF16)
        hidden_ref[:, at] = hidden
        slope = sigmoid_val * (1.0 + pre_act * (1.0 - sigmoid_val))
        hgrad_ref[:, at] = (back * slope).astype(BF16)
        score += jnp.sum(hidden.astype(F32) * back, axis=1, keepdims=True)
        for k, (ref, out) in enumerate(((hidden_ref, hidden_out), (hgrad_ref, hgrad_out))):
            leaving.append(pltpu.make_async_copy(ref.at[:, at], out.at[:, at], row_sems.at[k, j]))
            leaving[-1].start()

    size = group_size(ret_ref.shape[0])
    main, rest = packers(size)
    groups = [
        (slice(g * size * CAP, (g + 1) * size * CAP), slice(g * size * ROWS, (g + 1) * size * ROWS))
        for g in range(rows // (size * CAP))
    ]
    high = score.astype(BF16)
    low = (score - high.astype(F32)).astype(BF16)
    lane = iota((rows, 128), 1)
    extra = jnp.where(lane == 0, high.astype(F32), jnp.where(lane == 1, low.astype(F32), 0.0))
    extra = extra.astype(BF16)
    for source, target in groups:
        ret_ref[target, 3 * block :] = dot(main, extra[source]).astype(BF16)

    def leave(start, width, at):
        copy = pltpu.make_async_copy(
            ret_ref.at[:, start : start + width], ret_out.at[:, start : start + width], ret_sems.at[at]
        )
        copy.start()
        leaving.append(copy)

    leave(3 * block, 128, 0)
    whole = hgrad_ref[...]
    chunk = min(768, block)
    for n in range(block // chunk):
        at = slice(n * chunk, (n + 1) * chunk)
        last = dot(whole, w3[at, :], NT).astype(BF16)
        for part, weight in enumerate((w0, w1, w2)):
            here = dot(whole, weight[at, :], NT).astype(BF16)
            start = part * block + n * chunk
            for source, target in groups:
                ret_ref[target, start : start + chunk] = (
                    dot(main, here[source]) + dot(rest[part], last[source])
                ).astype(BF16)
            leave(start, chunk, 1 + 3 * n + part)
    for copy in leaving:
        copy.wait()


def expert(wholes, ups, backs, experts):
    rows, block = wholes[0].shape
    hidden_width = ups[0].shape[1]
    packed = (experts * ROWS, 3 * block + 128)
    steps, chunks = hidden_width // min(512, hidden_width), block // min(768, block)
    spec = pl.BlockSpec(memory_space=pltpu.VMEM)
    anywhere = pl.BlockSpec(memory_space=pl.ANY)
    return pl.pallas_call(
        expert_body,
        out_shape=[jax.ShapeDtypeStruct((rows, hidden_width), BF16)] * 2
        + [jax.ShapeDtypeStruct(packed, BF16)],
        in_specs=[spec] * 4 + [anywhere] * 9,
        out_specs=[anywhere] * 3,
        scratch_shapes=[pltpu.VMEM((block, hidden_width), BF16)] * 4
        + [pltpu.VMEM((rows, hidden_width), F32)]
        + [pltpu.VMEM((rows, hidden_width), BF16)] * 5
        + [pltpu.VMEM(packed, BF16)]
        + [
            pltpu.SemaphoreType.DMA((9, steps)),
            pltpu.SemaphoreType.DMA((2, steps)),
            pltpu.SemaphoreType.DMA((1 + 3 * chunks,)),
        ],
        compiler_params=vmem(60),
        cost_estimate=pl.CostEstimate(
            flops=20 * rows * block * hidden_width,
            bytes_accessed=24 * block * hidden_width,
            transcendentals=rows * hidden_width,
        ),
    )(*wholes, *ups, *backs)


def combine_body(place_ref, ids_ref, weight_ref, ret_ref, dtok_ref, droute_ref):
    rows_all = ret_ref.shape[0]
    count, width = dtok_ref.shape
    block = width // 4
    routes = slots(ids_ref[0:1, :], ids_ref[1:2, :])
    eye = iota((count, count), 0) == iota((count, count), 1)

    def col(row):
        return jnp.sum(jnp.where(eye, row, jnp.zeros_like(row)), axis=1, keepdims=True)

    across = iota((count, rows_all), 1)
    hits = [(across == col(row_of(route))).astype(BF16) for route in routes]
    main = hits[0] + hits[1]
    rests = [rest_of(route) for route in routes]
    rest_rows = [col(row) for row, _ in rests]
    rest_parts = [col(part) for _, part in rests]

    def put(delta, values):
        start = lax.rem(place_ref[0] + delta, 4) * block
        dtok_ref[:, pl.ds(pl.multiple_of(start, 128), block)] = values.astype(BF16)

    last = jnp.zeros((count, block), F32)
    for part in range(3):
        got = ret_ref[:, part * block : (part + 1) * block]
        put(part, dot(main, got))
        pick = sum(
            ((across == row) & (column == part)).astype(F32)
            for row, column in zip(rest_rows, rest_parts)
        ).astype(BF16)
        last += dot(pick, got)
    put(3, last)
    extra = ret_ref[:, 3 * block :]
    for k in range(2):
        pair = dot(hits[k], extra)
        score = pair[:, 0:1] + pair[:, 1:2]
        row = jnp.sum(jnp.where(eye, score, 0.0), axis=0, keepdims=True)
        droute_ref[k : k + 1, :] = (row / weight_ref[k : k + 1, :].astype(F32)).astype(BF16)


def combine(place, ids, weight, ret, count, width):
    spec = pl.BlockSpec(memory_space=pltpu.VMEM)
    return pl.pallas_call(
        combine_body,
        out_shape=[
            jax.ShapeDtypeStruct((count, width), BF16),
            jax.ShapeDtypeStruct((2, count), BF16),
        ],
        in_specs=[pl.BlockSpec(memory_space=pltpu.SMEM), spec, spec, spec],
        out_specs=[spec, spec],
        compiler_params=vmem(20),
        cost_estimate=pl.CostEstimate(
            flops=4 * ret.shape[0] * count * width,
            bytes_accessed=2 * (count * width + ret.size),
            transcendentals=0,
        ),
    )(place, ids, weight, ret)


def near_body(l0, l1, l3, r0, r1, r3, out_ref):
    step = min(256, out_ref.shape[0])

    def one(j, carry):
        at = pl.ds(pl.multiple_of(j * step, step), step)
        total = dot(l0[:, at], r0[...], TN)
        total += dot(l1[:, at], r1[...], TN)
        total += dot(l3[:, at], r3[...], TN)
        out_ref[at, :] = total
        return carry

    lax.fori_loop(0, out_ref.shape[0] // step, one, 0)


def outer_near(lefts, rights):
    rows, shape = lefts[0].shape[0], (lefts[0].shape[1], rights[0].shape[1])
    return pl.pallas_call(
        near_body,
        out_shape=jax.ShapeDtypeStruct(shape, F32),
        in_specs=[pl.BlockSpec(memory_space=pltpu.VMEM)] * 6,
        out_specs=pl.BlockSpec(memory_space=pltpu.VMEM),
        compiler_params=vmem(16),
        cost_estimate=pl.CostEstimate(
            flops=6 * rows * shape[0] * shape[1],
            bytes_accessed=6 * rows * sum(shape) + 4 * shape[0] * shape[1],
            transcendentals=0,
        ),
    )(*lefts, *rights)


def last_body(left_in_halves, total_ref, whole, first, second, out_ref):
    half = first.shape[0]
    step = min(256, out_ref.shape[0])

    def one(j, carry):
        at = pl.ds(pl.multiple_of(j * step, step), step)
        total = total_ref[at, :]
        if left_in_halves:
            total += dot(first[:, at], whole[:half, :], TN)
            total += dot(second[:, at], whole[half:, :], TN)
        else:
            total += dot(whole[:half, at], first[...], TN)
            total += dot(whole[half:, at], second[...], TN)
        out_ref[at, :] = total.astype(BF16)
        return carry

    lax.fori_loop(0, out_ref.shape[0] // step, one, 0)


def outer_last(left_in_halves, total, whole, first, second):
    return pl.pallas_call(
        functools.partial(last_body, left_in_halves),
        out_shape=jax.ShapeDtypeStruct(total.shape, BF16),
        in_specs=[pl.BlockSpec(memory_space=pltpu.VMEM)] * 4,
        out_specs=pl.BlockSpec(memory_space=pltpu.VMEM),
        compiler_params=vmem(16),
        cost_estimate=pl.CostEstimate(
            flops=2 * whole.shape[0] * total.shape[0] * total.shape[1],
            bytes_accessed=6 * total.size + 2 * whole.shape[0] * sum(total.shape),
            transcendentals=0,
        ),
    )(total, whole, first, second)


def shift(values, by):
    count = lax.axis_size("cross")
    return lax.ppermute(values, "cross", [(i, (i + by) % count) for i in range(count)])


def near(own):
    return own, shift(own, -1), shift(own, 1)


def far(pieces):
    own, after, before = pieces
    half = own.shape[0] // 2
    return own, after, shift(before[:half], 1), shift(after[half:], -1), before


def transpose(parts):
    return parts[0], shift(parts[3], -1), shift(parts[2], 2), shift(parts[1], 1)


def exchange(values, experts):
    blocks = values.reshape(experts, ROWS, values.shape[1])
    return lax.all_to_all(blocks, "expert", split_axis=0, concat_axis=0, tiled=True).reshape(
        values.shape
    )


def shards(tokens, route_ids, route_weight, cotangent, up_weight, down_weight):
    experts = lax.axis_size("expert")
    count, width = tokens.shape
    place = lax.axis_index("cross").astype(jnp.int32).reshape(1)
    ids, weight = route_ids.T, route_weight.T
    cot_slices = transpose(slices(place, ids, weight, cotangent))
    got_grad = exchange(dispatch_grads(cot_slices, experts), experts)
    ups_near = near(up_weight[0])
    sent_tokens = dispatch_tokens(place, ids, tokens, experts)
    sent_tokens, ups_near = lax.optimization_barrier((sent_tokens, ups_near))
    ups = far(ups_near)
    got_tokens = exchange(sent_tokens, experts)
    g0, g1, g2, g3, b0, b1, b2, b3 = project(got_grad, down_weight[0])
    backs = transpose((b0, b1, b2, b3))
    got_tokens, backs, ups = lax.optimization_barrier((got_tokens, backs, ups))
    wholes = unpack_rows(got_tokens)
    t1, t3 = shift(wholes[3], -1), shift(wholes[1], 1)
    hidden, hidden_grad, ret = expert(wholes, ups, backs, experts)
    ret, t1, t3 = lax.optimization_barrier((ret, t1, t3))
    back = exchange(ret, experts)
    h0, h1, h2a, h2b, h3 = far(near(hidden))
    down_near = outer_near((h0, h1, h3), (g0, g1, g3))
    grads_near, down_near, far_tokens = lax.optimization_barrier(
        (near(hidden_grad), down_near, wholes[2])
    )
    t2 = shift(far_tokens, 2)
    d0, d1, d2a, d2b, d3 = far(grads_near)
    up_near = outer_near((wholes[0], t1, t3), (d0, d1, d3))
    grad_down = outer_last(True, down_near, g2, h2a, h2b)
    back, grad_down, up_near = lax.optimization_barrier((back, grad_down, up_near))
    d_tokens, d_route = combine(place, ids, weight, back, count, width)
    up_near, d_tokens, d_route = lax.optimization_barrier((up_near, d_tokens, d_route))
    grad_up = outer_last(False, up_near, t2, d2a, d2b)
    return d_tokens, d_route.T, grad_up[None], grad_down[None]


def solution(mesh):
    rows = P(("expert", "cross"), None)
    ups, downs = P("expert", "cross", None), P("expert", None, "cross")
    return jax.shard_map(
        shards,
        mesh=mesh,
        in_specs=(rows, rows, rows, rows, ups, downs),
        out_specs=(rows, rows, ups, downs),
        check_vma=False,
    )
```

```python
import functools

import jax
import jax.numpy as jnp
from jax import lax
from jax.experimental import pallas as pl
from jax.experimental.pallas import tpu as pltpu
from jax.sharding import PartitionSpec as P

CAP = 6
ROWS = 8
F32 = jnp.float32
BF16 = jnp.bfloat16


def vmem(mebibytes):
    return pltpu.CompilerParams(vmem_limit_bytes=mebibytes * 1024 * 1024)


NT = (((1,), (1,)), ((), ()))
TN = (((0,), (0,)), ((), ()))


def iota(shape, dim):
    return lax.broadcasted_iota(jnp.int32, shape, dim)


def dot(a, b, dims=None):
    if dims is None:
        return jnp.dot(a, b, preferred_element_type=F32)
    return lax.dot_general(a, b, dims, preferred_element_type=F32)


def slots(first, second):
    count = first.shape[1]
    down, across = iota((count, count), 0), iota((count, count), 1)
    eye = down == across
    earlier = (down < across).astype(F32)
    first_col = jnp.sum(jnp.where(eye, first, 0), axis=1, keepdims=True)
    second_col = jnp.sum(jnp.where(eye, second, 0), axis=1, keepdims=True)

    def total(hits):
        return jnp.sum(hits, axis=0, keepdims=True)

    rank_first = total((first_col == first).astype(F32) * earlier)
    rank_second = total((first_col == second).astype(F32)) + total(
        (second_col == second).astype(F32) * earlier
    )
    return (first, rank_first.astype(jnp.int32)), (second, rank_second.astype(jnp.int32))


def row_of(route):
    return route[0] * ROWS + route[1]


def rest_of(route):
    late = (route[1] >= 3).astype(jnp.int32)
    return route[0] * ROWS + CAP + late, route[1] - 3 * late


def chosen(hit_of, routes, shares):
    return sum(
        jnp.where(hit_of(route), share, 0.0) for route, share in zip(routes, shares)
    ).astype(BF16)


def packed_block(down, part, mine, last):
    def hit_of(route):
        row, column = rest_of(route)
        return (down == row) & (column == part)

    main = chosen(lambda route: down == row_of(route), mine[0], mine[1])
    left = jnp.concatenate([main, chosen(hit_of, last[0], last[1])], axis=1)
    return dot(left, jnp.concatenate([mine[2], last[2]], axis=0)).astype(BF16)


def block_at(place_ref, ref, delta):
    block = ref.shape[1] // 4
    start = lax.rem(place_ref[0] + delta, 4) * block
    return ref[:, pl.ds(pl.multiple_of(start, 128), block)]


def token_body(place_ref, ids_ref, values_ref, out_ref):
    count, width = values_ref.shape
    block = width // 4
    down = iota((out_ref.shape[0], count), 0)
    routes = slots(ids_ref[0:1, :], ids_ref[1:2, :])
    shares = (1.0, 1.0)
    last = (routes, shares, block_at(place_ref, values_ref, 3))
    for part in range(3):
        mine = (routes, shares, block_at(place_ref, values_ref, part))
        out_ref[:, part * block : (part + 1) * block] = packed_block(down, part, mine, last)


def dispatch_tokens(place, ids, values, experts):
    count, width = values.shape
    rows_all = experts * ROWS
    packed = 3 * width // 4
    spec = pl.BlockSpec(memory_space=pltpu.VMEM)
    return pl.pallas_call(
        token_body,
        out_shape=jax.ShapeDtypeStruct((rows_all, packed), BF16),
        in_specs=[pl.BlockSpec(memory_space=pltpu.SMEM), spec, spec],
        out_specs=spec,
        compiler_params=vmem(60),
        cost_estimate=pl.CostEstimate(
            flops=4 * rows_all * count * packed,
            bytes_accessed=2 * (count * width + rows_all * packed),
            transcendentals=0,
        ),
    )(place, ids, values)


NOTES = 16


def slice_body(place_ref, ids_ref, weight_ref, values_ref, *out_refs):
    count, width = values_ref.shape
    block = width // 4
    row = iota((NOTES, count), 0)
    notes = jnp.zeros((NOTES, count), F32)
    for k in range(2):
        notes = jnp.where(row == k, ids_ref[k : k + 1, :].astype(F32), notes)
        notes = jnp.where(row == 2 + k, weight_ref[k : k + 1, :].astype(F32), notes)
    for delta, out_ref in enumerate(out_refs):
        out_ref[:count, :] = block_at(place_ref, values_ref, delta)
        out_ref[count:, :] = jnp.zeros((NOTES, block), BF16)
        out_ref[count:, :count] = notes.astype(BF16)


def slices(place, ids, weight, values):
    count, width = values.shape
    spec = pl.BlockSpec(memory_space=pltpu.VMEM)
    return pl.pallas_call(
        slice_body,
        out_shape=[jax.ShapeDtypeStruct((count + NOTES, width // 4), BF16)] * 4,
        in_specs=[pl.BlockSpec(memory_space=pltpu.SMEM), spec, spec, spec],
        out_specs=[spec] * 4,
        compiler_params=vmem(12),
        cost_estimate=pl.CostEstimate(
            flops=0, bytes_accessed=4 * count * width, transcendentals=0
        ),
    )(place, ids, weight, values)


def grad_body(s0, s1, s2, s3, out_ref):
    count = s0.shape[0] - NOTES
    block = s0.shape[1]
    down = iota((out_ref.shape[0], count), 0)
    groups = []
    for ref in (s0, s1, s2, s3):
        notes = ref[count:, :count].astype(F32)
        first, second = (notes[k : k + 1, :].astype(jnp.int32) for k in range(2))
        groups.append((slots(first, second), (notes[2:3, :], notes[3:4, :]), ref[:count, :]))
    for part in range(3):
        out_ref[:, part * block : (part + 1) * block] = packed_block(
            down, part, groups[part], groups[3]
        )


def dispatch_grads(parts, experts):
    count, block = parts[0].shape
    rows_all = experts * ROWS
    spec = pl.BlockSpec(memory_space=pltpu.VMEM)
    return pl.pallas_call(
        grad_body,
        out_shape=jax.ShapeDtypeStruct((rows_all, 3 * block), BF16),
        in_specs=[spec] * 4,
        out_specs=spec,
        compiler_params=vmem(16),
        cost_estimate=pl.CostEstimate(
            flops=12 * rows_all * count * block,
            bytes_accessed=2 * (4 * count + 3 * rows_all) * block,
            transcendentals=0,
        ),
    )(*parts)


def pickers(experts):
    rows, packed = experts * CAP, experts * ROWS
    at, column = iota((rows, packed), 0), iota((rows, packed), 1)
    expert = lax.shift_right_logical(at * 10923, 16)
    slot = at - expert * CAP
    late = (slot >= 3).astype(jnp.int32)
    main = (column == expert * ROWS + slot).astype(BF16)
    rest = [
        ((column == expert * ROWS + CAP + late) & (slot - 3 * late == part)).astype(BF16)
        for part in range(3)
    ]
    return main, rest


def packers(experts):
    rows, packed = experts * CAP, experts * ROWS
    at, column = iota((packed, rows), 1), iota((packed, rows), 0)
    expert = lax.shift_right_logical(at * 10923, 16)
    slot = at - expert * CAP
    late = (slot >= 3).astype(jnp.int32)
    main = (column == expert * ROWS + slot).astype(BF16)
    rest = [
        ((column == expert * ROWS + CAP + late) & (slot - 3 * late == part)).astype(BF16)
        for part in range(3)
    ]
    return main, rest


def group_size(rows_all):
    experts = rows_all // ROWS
    return min(32, experts)


def unpack(packed_ref, whole_refs):
    rows_all, packed = packed_ref.shape
    block = packed // 3
    size = group_size(rows_all)
    main, rest = pickers(size)
    for group in range(rows_all // (size * ROWS)):
        source = slice(group * size * ROWS, (group + 1) * size * ROWS)
        target = slice(group * size * CAP, (group + 1) * size * CAP)
        parts = [packed_ref[source, part * block : (part + 1) * block] for part in range(3)]
        for part in range(3):
            whole_refs[part][target, :] = dot(main, parts[part]).astype(BF16)
        whole_refs[3][target, :] = sum(dot(rest[part], parts[part]) for part in range(3)).astype(
            BF16
        )


def project_body(got_ref, down_ref, g0, g1, g2, g3, b0, b1, b2, b3):
    wholes = (g0, g1, g2, g3)
    unpack(got_ref, wholes)
    hidden_width = down_ref.shape[0]
    step = min(256, hidden_width)
    for j in range(hidden_width // step):
        at = slice(j * step, (j + 1) * step)
        weight = down_ref[at, :]
        for whole, out_ref in zip(wholes, (b0, b1, b2, b3)):
            out_ref[:, at] = dot(whole[...], weight, NT).astype(out_ref.dtype)


def project(got, down):
    rows_all, packed = got.shape
    rows = rows_all // ROWS * CAP
    block, hidden_width = packed // 3, down.shape[0]
    return pl.pallas_call(
        project_body,
        out_shape=[jax.ShapeDtypeStruct((rows, block), BF16)] * 4
        + [jax.ShapeDtypeStruct((rows, hidden_width), F32)]
        + [jax.ShapeDtypeStruct((rows, hidden_width), BF16)] * 3,
        in_specs=[pl.BlockSpec(memory_space=pltpu.VMEM)] * 2,
        out_specs=[pl.BlockSpec(memory_space=pltpu.VMEM)] * 8,
        compiler_params=vmem(60),
        cost_estimate=pl.CostEstimate(
            flops=10 * rows * block * hidden_width,
            bytes_accessed=12 * rows * (block + hidden_width),
            transcendentals=0,
        ),
    )(got, down)


def unpack_rows_body(got_ref, x0, x1, x2, x3):
    unpack(got_ref, (x0, x1, x2, x3))


def unpack_rows(got):
    rows_all, packed = got.shape
    size = group_size(rows_all)
    block = packed // 3
    return pl.pallas_call(
        unpack_rows_body,
        grid=(rows_all // (size * ROWS),),
        out_shape=[jax.ShapeDtypeStruct((rows_all // ROWS * CAP, block), BF16)] * 4,
        in_specs=[pl.BlockSpec((size * ROWS, packed), lambda i: (i, 0))],
        out_specs=[pl.BlockSpec((size * CAP, block), lambda i: (i, 0))] * 4,
        compiler_params=vmem(12),
        cost_estimate=pl.CostEstimate(
            flops=12 * rows_all * size * CAP * block,
            bytes_accessed=4 * rows_all * packed,
            transcendentals=0,
        ),
    )(got)


def expert_body(
    x0, x1, x2, x3, up0, up1, up2a, up2b, up3, b0, b1, b2, b3,
    hidden_out, hgrad_out, ret_out,
    w0, w1, w2, w3, p0, p1, p2, p3, hidden_ref, hgrad_ref, ret_ref, in_sems, row_sems, ret_sems,
):
    rows, hidden_width = hidden_ref.shape
    block = w0.shape[0]
    half = block // 2
    step = min(512, hidden_width)
    steps = hidden_width // step
    sources = (up0, up1, up2a, up2b, up3, b0, b1, b2, b3)
    places = (w0, w1, w2.at[:half, :], w2.at[half:, :], w3, p0, p1, p2, p3)

    def fetch(j):
        at = slice(j * step, (j + 1) * step)
        group = [
            pltpu.make_async_copy(source.at[:, at], place.at[:, at], in_sems.at[p, j])
            for p, (source, place) in enumerate(zip(sources, places))
        ]
        for copy in group:
            copy.start()
        return group

    fetched = [fetch(0)]
    leaving = []
    score = jnp.zeros((rows, 1), F32)
    for j in range(steps):
        at = slice(j * step, (j + 1) * step)
        if j + 1 < steps:
            fetched.append(fetch(j + 1))
        for copy in fetched[j]:
            copy.wait()
        pre_act = dot(x0[...], w0[:, at])
        pre_act += dot(x1[...], w1[:, at])
        pre_act += dot(x2[...], w2[:, at])
        pre_act += dot(x3[...], w3[:, at])
        back = p0[:, at] + p1[:, at].astype(F32) + p2[:, at].astype(F32) + p3[:, at].astype(F32)
        sigmoid_val = jax.nn.sigmoid(pre_act)
        hidden = (pre_act * sigmoid_val).astype(BF16)
        hidden_ref[:, at] = hidden
        slope = sigmoid_val * (1.0 + pre_act * (1.0 - sigmoid_val))
        hgrad_ref[:, at] = (back * slope).astype(BF16)
        score += jnp.sum(hidden.astype(F32) * back, axis=1, keepdims=True)
        for k, (ref, out) in enumerate(((hidden_ref, hidden_out), (hgrad_ref, hgrad_out))):
            leaving.append(pltpu.make_async_copy(ref.at[:, at], out.at[:, at], row_sems.at[k, j]))
            leaving[-1].start()

    size = group_size(ret_ref.shape[0])
    main, rest = packers(size)
    groups = [
        (slice(g * size * CAP, (g + 1) * size * CAP), slice(g * size * ROWS, (g + 1) * size * ROWS))
        for g in range(rows // (size * CAP))
    ]
    high = score.astype(BF16)
    low = (score - high.astype(F32)).astype(BF16)
    lane = iota((rows, 128), 1)
    extra = jnp.where(lane == 0, high.astype(F32), jnp.where(lane == 1, low.astype(F32), 0.0))
    extra = extra.astype(BF16)
    for source, target in groups:
        ret_ref[target, 3 * block :] = dot(main, extra[source]).astype(BF16)

    def leave(start, width, at):
        copy = pltpu.make_async_copy(
            ret_ref.at[:, start : start + width], ret_out.at[:, start : start + width], ret_sems.at[at]
        )
        copy.start()
        leaving.append(copy)

    leave(3 * block, 128, 0)
    whole = hgrad_ref[...]
    chunk = min(768, block)
    for n in range(block // chunk):
        at = slice(n * chunk, (n + 1) * chunk)
        last = dot(whole, w3[at, :], NT).astype(BF16)
        for part, weight in enumerate((w0, w1, w2)):
            here = dot(whole, weight[at, :], NT).astype(BF16)
            start = part * block + n * chunk
            for source, target in groups:
                ret_ref[target, start : start + chunk] = (
                    dot(main, here[source]) + dot(rest[part], last[source])
                ).astype(BF16)
            leave(start, chunk, 1 + 3 * n + part)
    for copy in leaving:
        copy.wait()


def expert(wholes, ups, backs, experts):
    rows, block = wholes[0].shape
    hidden_width = ups[0].shape[1]
    packed = (experts * ROWS, 3 * block + 128)
    steps, chunks = hidden_width // min(512, hidden_width), block // min(768, block)
    spec = pl.BlockSpec(memory_space=pltpu.VMEM)
    anywhere = pl.BlockSpec(memory_space=pl.ANY)
    return pl.pallas_call(
        expert_body,
        out_shape=[jax.ShapeDtypeStruct((rows, hidden_width), BF16)] * 2
        + [jax.ShapeDtypeStruct(packed, BF16)],
        in_specs=[spec] * 4 + [anywhere] * 9,
        out_specs=[anywhere] * 3,
        scratch_shapes=[pltpu.VMEM((block, hidden_width), BF16)] * 4
        + [pltpu.VMEM((rows, hidden_width), F32)]
        + [pltpu.VMEM((rows, hidden_width), BF16)] * 5
        + [pltpu.VMEM(packed, BF16)]
        + [
            pltpu.SemaphoreType.DMA((9, steps)),
            pltpu.SemaphoreType.DMA((2, steps)),
            pltpu.SemaphoreType.DMA((1 + 3 * chunks,)),
        ],
        compiler_params=vmem(63),
        cost_estimate=pl.CostEstimate(
            flops=20 * rows * block * hidden_width,
            bytes_accessed=24 * block * hidden_width,
            transcendentals=rows * hidden_width,
        ),
    )(*wholes, *ups, *backs)


def combine_body(place_ref, ids_ref, weight_ref, ret_ref, dtok_ref, droute_ref):
    rows_all = ret_ref.shape[0]
    count, width = dtok_ref.shape
    block = width // 4
    routes = slots(ids_ref[0:1, :], ids_ref[1:2, :])
    eye = iota((count, count), 0) == iota((count, count), 1)

    def col(row):
        return jnp.sum(jnp.where(eye, row, jnp.zeros_like(row)), axis=1, keepdims=True)

    across = iota((count, rows_all), 1)
    hits = [(across == col(row_of(route))).astype(BF16) for route in routes]
    main = hits[0] + hits[1]
    rests = [rest_of(route) for route in routes]
    rest_rows = [col(row) for row, _ in rests]
    rest_parts = [col(part) for _, part in rests]

    def put(delta, values):
        start = lax.rem(place_ref[0] + delta, 4) * block
        dtok_ref[:, pl.ds(pl.multiple_of(start, 128), block)] = values.astype(BF16)

    last = jnp.zeros((count, block), F32)
    for part in range(3):
        got = ret_ref[:, part * block : (part + 1) * block]
        put(part, dot(main, got))
        pick = sum(
            ((across == row) & (column == part)).astype(F32)
            for row, column in zip(rest_rows, rest_parts)
        ).astype(BF16)
        last += dot(pick, got)
    put(3, last)
    extra = ret_ref[:, 3 * block :]
    for k in range(2):
        pair = dot(hits[k], extra)
        score = pair[:, 0:1] + pair[:, 1:2]
        row = jnp.sum(jnp.where(eye, score, 0.0), axis=0, keepdims=True)
        droute_ref[k : k + 1, :] = (row / weight_ref[k : k + 1, :].astype(F32)).astype(BF16)


def combine(place, ids, weight, ret, count, width):
    spec = pl.BlockSpec(memory_space=pltpu.VMEM)
    return pl.pallas_call(
        combine_body,
        out_shape=[
            jax.ShapeDtypeStruct((count, width), BF16),
            jax.ShapeDtypeStruct((2, count), BF16),
        ],
        in_specs=[pl.BlockSpec(memory_space=pltpu.SMEM), spec, spec, spec],
        out_specs=[spec, spec],
        compiler_params=vmem(20),
        cost_estimate=pl.CostEstimate(
            flops=4 * ret.shape[0] * count * width,
            bytes_accessed=2 * (count * width + ret.size),
            transcendentals=0,
        ),
    )(place, ids, weight, ret)


def near_body(l0, l1, l3, r0, r1, r3, out_ref):
    step = min(256, out_ref.shape[0])

    def one(j, carry):
        at = pl.ds(pl.multiple_of(j * step, step), step)
        total = dot(l0[:, at], r0[...], TN)
        total += dot(l1[:, at], r1[...], TN)
        total += dot(l3[:, at], r3[...], TN)
        out_ref[at, :] = total
        return carry

    lax.fori_loop(0, out_ref.shape[0] // step, one, 0)


def outer_near(lefts, rights):
    rows, shape = lefts[0].shape[0], (lefts[0].shape[1], rights[0].shape[1])
    return pl.pallas_call(
        near_body,
        out_shape=jax.ShapeDtypeStruct(shape, F32),
        in_specs=[pl.BlockSpec(memory_space=pltpu.VMEM)] * 6,
        out_specs=pl.BlockSpec(memory_space=pltpu.VMEM),
        compiler_params=vmem(16),
        cost_estimate=pl.CostEstimate(
            flops=6 * rows * shape[0] * shape[1],
            bytes_accessed=6 * rows * sum(shape) + 4 * shape[0] * shape[1],
            transcendentals=0,
        ),
    )(*lefts, *rights)


def last_body(left_in_halves, total_ref, whole, first, second, out_ref):
    half = first.shape[0]
    step = min(256, out_ref.shape[0])

    def one(j, carry):
        at = pl.ds(pl.multiple_of(j * step, step), step)
        total = total_ref[at, :]
        if left_in_halves:
            total += dot(first[:, at], whole[:half, :], TN)
            total += dot(second[:, at], whole[half:, :], TN)
        else:
            total += dot(whole[:half, at], first[...], TN)
            total += dot(whole[half:, at], second[...], TN)
        out_ref[at, :] = total.astype(BF16)
        return carry

    lax.fori_loop(0, out_ref.shape[0] // step, one, 0)


def outer_last(left_in_halves, total, whole, first, second):
    return pl.pallas_call(
        functools.partial(last_body, left_in_halves),
        out_shape=jax.ShapeDtypeStruct(total.shape, BF16),
        in_specs=[pl.BlockSpec(memory_space=pltpu.VMEM)] * 4,
        out_specs=pl.BlockSpec(memory_space=pltpu.VMEM),
        compiler_params=vmem(16),
        cost_estimate=pl.CostEstimate(
            flops=2 * whole.shape[0] * total.shape[0] * total.shape[1],
            bytes_accessed=6 * total.size + 2 * whole.shape[0] * sum(total.shape),
            transcendentals=0,
        ),
    )(total, whole, first, second)


def shift(values, by):
    count = lax.axis_size("cross")
    return lax.ppermute(values, "cross", [(i, (i + by) % count) for i in range(count)])


def near(own):
    return own, shift(own, -1), shift(own, 1)


def far(pieces):
    own, after, before = pieces
    half = own.shape[0] // 2
    return own, after, shift(before[:half], 1), shift(after[half:], -1), before


def transpose(parts):
    return parts[0], shift(parts[3], -1), shift(parts[2], 2), shift(parts[1], 1)


def exchange(values, experts):
    blocks = values.reshape(experts, ROWS, values.shape[1])
    return lax.all_to_all(blocks, "expert", split_axis=0, concat_axis=0, tiled=True).reshape(
        values.shape
    )


def shards(tokens, route_ids, route_weight, cotangent, up_weight, down_weight):
    experts = lax.axis_size("expert")
    count, width = tokens.shape
    place = lax.axis_index("cross").astype(jnp.int32).reshape(1)
    ids, weight = route_ids.T, route_weight.T
    cot_slices = transpose(slices(place, ids, weight, cotangent))
    got_grad = exchange(dispatch_grads(cot_slices, experts), experts)
    ups_near = near(up_weight[0])
    sent_tokens = dispatch_tokens(place, ids, tokens, experts)
    sent_tokens, ups_near = lax.optimization_barrier((sent_tokens, ups_near))
    ups = far(ups_near)
    got_tokens = exchange(sent_tokens, experts)
    g0, g1, g2, g3, b0, b1, b2, b3 = project(got_grad, down_weight[0])
    backs = transpose((b0, b1, b2, b3))
    got_tokens, backs, ups = lax.optimization_barrier((got_tokens, backs, ups))
    wholes = unpack_rows(got_tokens)
    t1, t3 = shift(wholes[3], -1), shift(wholes[1], 1)
    hidden, hidden_grad, ret = expert(wholes, ups, backs, experts)
    ret, t1, t3 = lax.optimization_barrier((ret, t1, t3))
    back = exchange(ret, experts)
    hidden_near, far_tokens = lax.optimization_barrier((near(hidden), wholes[2]))
    h0, h1, h2a, h2b, h3 = far(hidden_near)
    t2 = shift(far_tokens, 2)
    down_near = outer_near((h0, h1, h3), (g0, g1, g3))
    grads_near, down_near = lax.optimization_barrier((near(hidden_grad), down_near))
    d0, d1, d2a, d2b, d3 = far(grads_near)
    up_near = outer_near((wholes[0], t1, t3), (d0, d1, d3))
    grad_down = outer_last(True, down_near, g2, h2a, h2b)
    back, grad_down, up_near = lax.optimization_barrier((back, grad_down, up_near))
    d_tokens, d_route = combine(place, ids, weight, back, count, width)
    up_near, d_tokens, d_route = lax.optimization_barrier((up_near, d_tokens, d_route))
    grad_up = outer_last(False, up_near, t2, d2a, d2b)
    return d_tokens, d_route.T, grad_up[None], grad_down[None]


def solution(mesh):
    rows = P(("expert", "cross"), None)
    ups, downs = P("expert", "cross", None), P("expert", None, "cross")
    return jax.shard_map(
        shards,
        mesh=mesh,
        in_specs=(rows, rows, rows, rows, ups, downs),
        out_specs=(rows, rows, ups, downs),
        check_vma=False,
    )
```

```python
import functools

import jax
import jax.numpy as jnp
from jax import lax
from jax.experimental import pallas as pl
from jax.experimental.pallas import tpu as pltpu
from jax.sharding import PartitionSpec as P

CAP = 6
ROWS = 8
F32 = jnp.float32
BF16 = jnp.bfloat16


def vmem(mebibytes):
    return pltpu.CompilerParams(vmem_limit_bytes=mebibytes * 1024 * 1024)


NT = (((1,), (1,)), ((), ()))
TN = (((0,), (0,)), ((), ()))


def iota(shape, dim):
    return lax.broadcasted_iota(jnp.int32, shape, dim)


def dot(a, b, dims=None):
    if dims is None:
        return jnp.dot(a, b, preferred_element_type=F32)
    return lax.dot_general(a, b, dims, preferred_element_type=F32)


def slots(first, second):
    count = first.shape[1]
    down, across = iota((count, count), 0), iota((count, count), 1)
    eye = down == across
    earlier = (down < across).astype(F32)
    first_col = jnp.sum(jnp.where(eye, first, 0), axis=1, keepdims=True)
    second_col = jnp.sum(jnp.where(eye, second, 0), axis=1, keepdims=True)

    def total(hits):
        return jnp.sum(hits, axis=0, keepdims=True)

    rank_first = total((first_col == first).astype(F32) * earlier)
    rank_second = total((first_col == second).astype(F32)) + total(
        (second_col == second).astype(F32) * earlier
    )
    return (first, rank_first.astype(jnp.int32)), (second, rank_second.astype(jnp.int32))


def row_of(route):
    return route[0] * ROWS + route[1]


def rest_of(route):
    late = (route[1] >= 3).astype(jnp.int32)
    return route[0] * ROWS + CAP + late, route[1] - 3 * late


def chosen(hit_of, routes, shares):
    return sum(
        jnp.where(hit_of(route), share, 0.0) for route, share in zip(routes, shares)
    ).astype(BF16)


def packed_block(down, part, mine, last):
    def hit_of(route):
        row, column = rest_of(route)
        return (down == row) & (column == part)

    main = chosen(lambda route: down == row_of(route), mine[0], mine[1])
    left = jnp.concatenate([main, chosen(hit_of, last[0], last[1])], axis=1)
    return dot(left, jnp.concatenate([mine[2], last[2]], axis=0)).astype(BF16)


def block_at(place_ref, ref, delta):
    block = ref.shape[1] // 4
    start = lax.rem(place_ref[0] + delta, 4) * block
    return ref[:, pl.ds(pl.multiple_of(start, 128), block)]


def token_body(place_ref, ids_ref, values_ref, out_ref):
    count, width = values_ref.shape
    block = width // 4
    down = iota((out_ref.shape[0], count), 0)
    routes = slots(ids_ref[0:1, :], ids_ref[1:2, :])
    shares = (1.0, 1.0)
    last = (routes, shares, block_at(place_ref, values_ref, 3))
    for part in range(3):
        mine = (routes, shares, block_at(place_ref, values_ref, part))
        out_ref[:, part * block : (part + 1) * block] = packed_block(down, part, mine, last)


def dispatch_tokens(place, ids, values, experts):
    count, width = values.shape
    rows_all = experts * ROWS
    packed = 3 * width // 4
    spec = pl.BlockSpec(memory_space=pltpu.VMEM)
    return pl.pallas_call(
        token_body,
        out_shape=jax.ShapeDtypeStruct((rows_all, packed), BF16),
        in_specs=[pl.BlockSpec(memory_space=pltpu.SMEM), spec, spec],
        out_specs=spec,
        compiler_params=vmem(60),
        cost_estimate=pl.CostEstimate(
            flops=4 * rows_all * count * packed,
            bytes_accessed=2 * (count * width + rows_all * packed),
            transcendentals=0,
        ),
    )(place, ids, values)


NOTES = 16


def slice_body(place_ref, ids_ref, weight_ref, values_ref, *out_refs):
    count, width = values_ref.shape
    block = width // 4
    row = iota((NOTES, count), 0)
    notes = jnp.zeros((NOTES, count), F32)
    for k in range(2):
        notes = jnp.where(row == k, ids_ref[k : k + 1, :].astype(F32), notes)
        notes = jnp.where(row == 2 + k, weight_ref[k : k + 1, :].astype(F32), notes)
    for delta, out_ref in enumerate(out_refs):
        out_ref[:count, :] = block_at(place_ref, values_ref, delta)
        out_ref[count:, :] = jnp.zeros((NOTES, block), BF16)
        out_ref[count:, :count] = notes.astype(BF16)


def slices(place, ids, weight, values):
    count, width = values.shape
    spec = pl.BlockSpec(memory_space=pltpu.VMEM)
    return pl.pallas_call(
        slice_body,
        out_shape=[jax.ShapeDtypeStruct((count + NOTES, width // 4), BF16)] * 4,
        in_specs=[pl.BlockSpec(memory_space=pltpu.SMEM), spec, spec, spec],
        out_specs=[spec] * 4,
        compiler_params=vmem(12),
        cost_estimate=pl.CostEstimate(
            flops=0, bytes_accessed=4 * count * width, transcendentals=0
        ),
    )(place, ids, weight, values)


def grad_body(s0, s1, s2, s3, out_ref):
    count = s0.shape[0] - NOTES
    block = s0.shape[1]
    down = iota((out_ref.shape[0], count), 0)
    groups = []
    for ref in (s0, s1, s2, s3):
        notes = ref[count:, :count].astype(F32)
        first, second = (notes[k : k + 1, :].astype(jnp.int32) for k in range(2))
        groups.append((slots(first, second), (notes[2:3, :], notes[3:4, :]), ref[:count, :]))
    for part in range(3):
        out_ref[:, part * block : (part + 1) * block] = packed_block(
            down, part, groups[part], groups[3]
        )


def dispatch_grads(parts, experts):
    count, block = parts[0].shape
    rows_all = experts * ROWS
    spec = pl.BlockSpec(memory_space=pltpu.VMEM)
    return pl.pallas_call(
        grad_body,
        out_shape=jax.ShapeDtypeStruct((rows_all, 3 * block), BF16),
        in_specs=[spec] * 4,
        out_specs=spec,
        compiler_params=vmem(16),
        cost_estimate=pl.CostEstimate(
            flops=12 * rows_all * count * block,
            bytes_accessed=2 * (4 * count + 3 * rows_all) * block,
            transcendentals=0,
        ),
    )(*parts)


def pickers(experts):
    rows, packed = experts * CAP, experts * ROWS
    at, column = iota((rows, packed), 0), iota((rows, packed), 1)
    expert = lax.shift_right_logical(at * 10923, 16)
    slot = at - expert * CAP
    late = (slot >= 3).astype(jnp.int32)
    main = (column == expert * ROWS + slot).astype(BF16)
    rest = [
        ((column == expert * ROWS + CAP + late) & (slot - 3 * late == part)).astype(BF16)
        for part in range(3)
    ]
    return main, rest


def packers(experts):
    rows, packed = experts * CAP, experts * ROWS
    at, column = iota((packed, rows), 1), iota((packed, rows), 0)
    expert = lax.shift_right_logical(at * 10923, 16)
    slot = at - expert * CAP
    late = (slot >= 3).astype(jnp.int32)
    main = (column == expert * ROWS + slot).astype(BF16)
    rest = [
        ((column == expert * ROWS + CAP + late) & (slot - 3 * late == part)).astype(BF16)
        for part in range(3)
    ]
    return main, rest


def group_size(rows_all):
    experts = rows_all // ROWS
    return min(32, experts)


def unpack(packed_ref, whole_refs):
    rows_all, packed = packed_ref.shape
    block = packed // 3
    size = group_size(rows_all)
    main, rest = pickers(size)
    for group in range(rows_all // (size * ROWS)):
        source = slice(group * size * ROWS, (group + 1) * size * ROWS)
        target = slice(group * size * CAP, (group + 1) * size * CAP)
        parts = [packed_ref[source, part * block : (part + 1) * block] for part in range(3)]
        for part in range(3):
            whole_refs[part][target, :] = dot(main, parts[part]).astype(BF16)
        whole_refs[3][target, :] = sum(dot(rest[part], parts[part]) for part in range(3)).astype(
            BF16
        )


def project_body(got_ref, down_ref, g0, g1, g2, g3, b0, b1, b2, b3):
    wholes = (g0, g1, g2, g3)
    unpack(got_ref, wholes)
    hidden_width = down_ref.shape[0]
    step = min(256, hidden_width)
    for j in range(hidden_width // step):
        at = slice(j * step, (j + 1) * step)
        weight = down_ref[at, :]
        for whole, out_ref in zip(wholes, (b0, b1, b2, b3)):
            out_ref[:, at] = dot(whole[...], weight, NT).astype(out_ref.dtype)


def project(got, down):
    rows_all, packed = got.shape
    rows = rows_all // ROWS * CAP
    block, hidden_width = packed // 3, down.shape[0]
    return pl.pallas_call(
        project_body,
        out_shape=[jax.ShapeDtypeStruct((rows, block), BF16)] * 4
        + [jax.ShapeDtypeStruct((rows, hidden_width), F32)]
        + [jax.ShapeDtypeStruct((rows, hidden_width), BF16)] * 3,
        in_specs=[pl.BlockSpec(memory_space=pltpu.VMEM)] * 2,
        out_specs=[pl.BlockSpec(memory_space=pltpu.VMEM)] * 8,
        compiler_params=vmem(60),
        cost_estimate=pl.CostEstimate(
            flops=10 * rows * block * hidden_width,
            bytes_accessed=12 * rows * (block + hidden_width),
            transcendentals=0,
        ),
    )(got, down)


def unpack_rows_body(got_ref, x0, x1, x2, x3):
    unpack(got_ref, (x0, x1, x2, x3))


def unpack_rows(got):
    rows_all, packed = got.shape
    size = group_size(rows_all)
    block = packed // 3
    return pl.pallas_call(
        unpack_rows_body,
        grid=(rows_all // (size * ROWS),),
        out_shape=[jax.ShapeDtypeStruct((rows_all // ROWS * CAP, block), BF16)] * 4,
        in_specs=[pl.BlockSpec((size * ROWS, packed), lambda i: (i, 0))],
        out_specs=[pl.BlockSpec((size * CAP, block), lambda i: (i, 0))] * 4,
        compiler_params=vmem(12),
        cost_estimate=pl.CostEstimate(
            flops=12 * rows_all * size * CAP * block,
            bytes_accessed=4 * rows_all * packed,
            transcendentals=0,
        ),
    )(got)


def expert_body(
    x0, x1, x2, x3, up0, up1, up2a, up2b, up3, b0, b1, b2, b3,
    hidden_out, hgrad_out, ret_out,
    w0, w1, w2, w3, p0, p1, p2, p3, hidden_ref, hgrad_ref, ret_ref, in_sems, row_sems, ret_sems,
):
    rows, hidden_width = hidden_ref.shape
    block = w0.shape[0]
    half = block // 2
    step = min(512, hidden_width)
    steps = hidden_width // step
    sources = (up0, up1, up2a, up2b, up3, b0, b1, b2, b3)
    places = (w0, w1, w2.at[:half, :], w2.at[half:, :], w3, p0, p1, p2, p3)

    def fetch(j):
        at = slice(j * step, (j + 1) * step)
        group = [
            pltpu.make_async_copy(source.at[:, at], place.at[:, at], in_sems.at[p, j])
            for p, (source, place) in enumerate(zip(sources, places))
        ]
        for copy in group:
            copy.start()
        return group

    fetched = [fetch(0)]
    leaving = []
    score = jnp.zeros((rows, 1), F32)
    for j in range(steps):
        at = slice(j * step, (j + 1) * step)
        if j + 1 < steps:
            fetched.append(fetch(j + 1))
        for copy in fetched[j]:
            copy.wait()
        pre_act = dot(x0[...], w0[:, at])
        pre_act += dot(x1[...], w1[:, at])
        pre_act += dot(x2[...], w2[:, at])
        pre_act += dot(x3[...], w3[:, at])
        back = p0[:, at] + p1[:, at].astype(F32) + p2[:, at].astype(F32) + p3[:, at].astype(F32)
        sigmoid_val = jax.nn.sigmoid(pre_act)
        hidden = (pre_act * sigmoid_val).astype(BF16)
        hidden_ref[:, at] = hidden
        slope = sigmoid_val * (1.0 + pre_act * (1.0 - sigmoid_val))
        hgrad_ref[:, at] = (back * slope).astype(BF16)
        score += jnp.sum(hidden.astype(F32) * back, axis=1, keepdims=True)
        for k, (ref, out) in enumerate(((hidden_ref, hidden_out), (hgrad_ref, hgrad_out))):
            leaving.append(pltpu.make_async_copy(ref.at[:, at], out.at[:, at], row_sems.at[k, j]))
            leaving[-1].start()

    size = group_size(ret_ref.shape[0])
    main, rest = packers(size)
    groups = [
        (slice(g * size * CAP, (g + 1) * size * CAP), slice(g * size * ROWS, (g + 1) * size * ROWS))
        for g in range(rows // (size * CAP))
    ]
    high = score.astype(BF16)
    low = (score - high.astype(F32)).astype(BF16)
    lane = iota((rows, 128), 1)
    extra = jnp.where(lane == 0, high.astype(F32), jnp.where(lane == 1, low.astype(F32), 0.0))
    extra = extra.astype(BF16)
    for source, target in groups:
        ret_ref[target, 3 * block :] = dot(main, extra[source]).astype(BF16)

    def leave(start, width, at):
        copy = pltpu.make_async_copy(
            ret_ref.at[:, start : start + width], ret_out.at[:, start : start + width], ret_sems.at[at]
        )
        copy.start()
        leaving.append(copy)

    leave(3 * block, 128, 0)
    whole = hgrad_ref[...]
    chunk = min(768, block)
    for n in range(block // chunk):
        at = slice(n * chunk, (n + 1) * chunk)
        last = dot(whole, w3[at, :], NT).astype(BF16)
        for part, weight in enumerate((w0, w1, w2)):
            here = dot(whole, weight[at, :], NT).astype(BF16)
            start = part * block + n * chunk
            for source, target in groups:
                ret_ref[target, start : start + chunk] = (
                    dot(main, here[source]) + dot(rest[part], last[source])
                ).astype(BF16)
            leave(start, chunk, 1 + 3 * n + part)
    for copy in leaving:
        copy.wait()


def expert(wholes, ups, backs, experts):
    rows, block = wholes[0].shape
    hidden_width = ups[0].shape[1]
    packed = (experts * ROWS, 3 * block + 128)
    steps, chunks = hidden_width // min(512, hidden_width), block // min(768, block)
    spec = pl.BlockSpec(memory_space=pltpu.VMEM)
    anywhere = pl.BlockSpec(memory_space=pl.ANY)
    return pl.pallas_call(
        expert_body,
        out_shape=[jax.ShapeDtypeStruct((rows, hidden_width), BF16)] * 2
        + [jax.ShapeDtypeStruct(packed, BF16)],
        in_specs=[spec] * 4 + [anywhere] * 9,
        out_specs=[anywhere] * 3,
        scratch_shapes=[pltpu.VMEM((block, hidden_width), BF16)] * 4
        + [pltpu.VMEM((rows, hidden_width), F32)]
        + [pltpu.VMEM((rows, hidden_width), BF16)] * 5
        + [pltpu.VMEM(packed, BF16)]
        + [
            pltpu.SemaphoreType.DMA((9, steps)),
            pltpu.SemaphoreType.DMA((2, steps)),
            pltpu.SemaphoreType.DMA((1 + 3 * chunks,)),
        ],
        compiler_params=vmem(63),
        cost_estimate=pl.CostEstimate(
            flops=20 * rows * block * hidden_width,
            bytes_accessed=24 * block * hidden_width,
            transcendentals=rows * hidden_width,
        ),
    )(*wholes, *ups, *backs)


def combine_body(place_ref, ids_ref, weight_ref, ret_ref, dtok_ref, droute_ref):
    rows_all = ret_ref.shape[0]
    count, width = dtok_ref.shape
    block = width // 4
    routes = slots(ids_ref[0:1, :], ids_ref[1:2, :])
    eye = iota((count, count), 0) == iota((count, count), 1)

    def col(row):
        return jnp.sum(jnp.where(eye, row, jnp.zeros_like(row)), axis=1, keepdims=True)

    across = iota((count, rows_all), 1)
    hits = [(across == col(row_of(route))).astype(BF16) for route in routes]
    main = hits[0] + hits[1]
    rests = [rest_of(route) for route in routes]
    rest_rows = [col(row) for row, _ in rests]
    rest_parts = [col(part) for _, part in rests]

    def put(delta, values):
        start = lax.rem(place_ref[0] + delta, 4) * block
        dtok_ref[:, pl.ds(pl.multiple_of(start, 128), block)] = values.astype(BF16)

    last = jnp.zeros((count, block), F32)
    for part in range(3):
        got = ret_ref[:, part * block : (part + 1) * block]
        put(part, dot(main, got))
        pick = sum(
            ((across == row) & (column == part)).astype(F32)
            for row, column in zip(rest_rows, rest_parts)
        ).astype(BF16)
        last += dot(pick, got)
    put(3, last)
    extra = ret_ref[:, 3 * block :]
    choice = iota((2, count), 0)
    out = jnp.zeros((2, count), F32)
    for k in range(2):
        pair = dot(hits[k], extra)
        score = pair[:, 0:1] + pair[:, 1:2]
        row = jnp.sum(jnp.where(eye, score, 0.0), axis=0, keepdims=True)
        out = jnp.where(choice == k, row, out)
    droute_ref[...] = (out / weight_ref[...].astype(F32)).astype(BF16)


def combine(place, ids, weight, ret, count, width):
    spec = pl.BlockSpec(memory_space=pltpu.VMEM)
    return pl.pallas_call(
        combine_body,
        out_shape=[
            jax.ShapeDtypeStruct((count, width), BF16),
            jax.ShapeDtypeStruct((2, count), BF16),
        ],
        in_specs=[pl.BlockSpec(memory_space=pltpu.SMEM), spec, spec, spec],
        out_specs=[spec, spec],
        compiler_params=vmem(20),
        cost_estimate=pl.CostEstimate(
            flops=4 * ret.shape[0] * count * width,
            bytes_accessed=2 * (count * width + ret.size),
            transcendentals=0,
        ),
    )(place, ids, weight, ret)


def near_body(l0, l1, l3, r0, r1, r3, out_ref):
    step = min(256, out_ref.shape[0])

    def one(j, carry):
        at = pl.ds(pl.multiple_of(j * step, step), step)
        total = dot(l0[:, at], r0[...], TN)
        total += dot(l1[:, at], r1[...], TN)
        total += dot(l3[:, at], r3[...], TN)
        out_ref[at, :] = total
        return carry

    lax.fori_loop(0, out_ref.shape[0] // step, one, 0)


def outer_near(lefts, rights):
    rows, shape = lefts[0].shape[0], (lefts[0].shape[1], rights[0].shape[1])
    return pl.pallas_call(
        near_body,
        out_shape=jax.ShapeDtypeStruct(shape, F32),
        in_specs=[pl.BlockSpec(memory_space=pltpu.VMEM)] * 6,
        out_specs=pl.BlockSpec(memory_space=pltpu.VMEM),
        compiler_params=vmem(16),
        cost_estimate=pl.CostEstimate(
            flops=6 * rows * shape[0] * shape[1],
            bytes_accessed=6 * rows * sum(shape) + 4 * shape[0] * shape[1],
            transcendentals=0,
        ),
    )(*lefts, *rights)


def last_body(left_in_halves, total_ref, whole, first, second, out_ref):
    half = first.shape[0]
    step = min(256, out_ref.shape[0])

    def one(j, carry):
        at = pl.ds(pl.multiple_of(j * step, step), step)
        total = total_ref[at, :]
        if left_in_halves:
            total += dot(first[:, at], whole[:half, :], TN)
            total += dot(second[:, at], whole[half:, :], TN)
        else:
            total += dot(whole[:half, at], first[...], TN)
            total += dot(whole[half:, at], second[...], TN)
        out_ref[at, :] = total.astype(BF16)
        return carry

    lax.fori_loop(0, out_ref.shape[0] // step, one, 0)


def outer_last(left_in_halves, total, whole, first, second):
    return pl.pallas_call(
        functools.partial(last_body, left_in_halves),
        out_shape=jax.ShapeDtypeStruct(total.shape, BF16),
        in_specs=[pl.BlockSpec(memory_space=pltpu.VMEM)] * 4,
        out_specs=pl.BlockSpec(memory_space=pltpu.VMEM),
        compiler_params=vmem(16),
        cost_estimate=pl.CostEstimate(
            flops=2 * whole.shape[0] * total.shape[0] * total.shape[1],
            bytes_accessed=6 * total.size + 2 * whole.shape[0] * sum(total.shape),
            transcendentals=0,
        ),
    )(total, whole, first, second)


def shift(values, by):
    count = lax.axis_size("cross")
    return lax.ppermute(values, "cross", [(i, (i + by) % count) for i in range(count)])


def near(own):
    return own, shift(own, -1), shift(own, 1)


def far(pieces):
    own, after, before = pieces
    half = own.shape[0] // 2
    return own, after, shift(before[:half], 1), shift(after[half:], -1), before


def transpose(parts):
    return parts[0], shift(parts[3], -1), shift(parts[2], 2), shift(parts[1], 1)


def exchange(values, experts):
    blocks = values.reshape(experts, ROWS, values.shape[1])
    return lax.all_to_all(blocks, "expert", split_axis=0, concat_axis=0, tiled=True).reshape(
        values.shape
    )


def shards(tokens, route_ids, route_weight, cotangent, up_weight, down_weight):
    experts = lax.axis_size("expert")
    count, width = tokens.shape
    place = lax.axis_index("cross").astype(jnp.int32).reshape(1)
    ids, weight = route_ids.T, route_weight.T
    cot_slices = transpose(slices(place, ids, weight, cotangent))
    got_grad = exchange(dispatch_grads(cot_slices, experts), experts)
    ups_near = near(up_weight[0])
    sent_tokens = dispatch_tokens(place, ids, tokens, experts)
    sent_tokens, ups_near = lax.optimization_barrier((sent_tokens, ups_near))
    ups = far(ups_near)
    got_tokens = exchange(sent_tokens, experts)
    g0, g1, g2, g3, b0, b1, b2, b3 = project(got_grad, down_weight[0])
    backs = transpose((b0, b1, b2, b3))
    got_tokens, backs, ups = lax.optimization_barrier((got_tokens, backs, ups))
    wholes = unpack_rows(got_tokens)
    t1, t3 = shift(wholes[3], -1), shift(wholes[1], 1)
    hidden, hidden_grad, ret = expert(wholes, ups, backs, experts)
    ret, t1, t3 = lax.optimization_barrier((ret, t1, t3))
    back = exchange(ret, experts)
    hidden_near, far_tokens = lax.optimization_barrier((near(hidden), wholes[2]))
    h0, h1, h2a, h2b, h3 = far(hidden_near)
    t2 = shift(far_tokens, 2)
    down_near = outer_near((h0, h1, h3), (g0, g1, g3))
    grad_down = outer_last(True, down_near, g2, h2a, h2b)
    grads_near, grad_down = lax.optimization_barrier((near(hidden_grad), grad_down))
    d0, d1, d2a, d2b, d3 = far(grads_near)
    up_near = outer_near((wholes[0], t1, t3), (d0, d1, d3))
    back, up_near = lax.optimization_barrier((back, up_near))
    d_tokens, d_route = combine(place, ids, weight, back, count, width)
    up_near, d_tokens, d_route = lax.optimization_barrier((up_near, d_tokens, d_route))
    grad_up = outer_last(False, up_near, t2, d2a, d2b)
    return d_tokens, d_route.T, grad_up[None], grad_down[None]


def solution(mesh):
    rows = P(("expert", "cross"), None)
    ups, downs = P("expert", "cross", None), P("expert", None, "cross")
    return jax.shard_map(
        shards,
        mesh=mesh,
        in_specs=(rows, rows, rows, rows, ups, downs),
        out_specs=(rows, rows, ups, downs),
        check_vma=False,
    )
```

```python
import functools

import jax
import jax.numpy as jnp
from jax import lax
from jax.experimental import pallas as pl
from jax.experimental.pallas import tpu as pltpu
from jax.sharding import PartitionSpec as P

CAP = 6
ROWS = 8
F32 = jnp.float32
BF16 = jnp.bfloat16


def vmem(mebibytes):
    return pltpu.CompilerParams(vmem_limit_bytes=mebibytes * 1024 * 1024)


NT = (((1,), (1,)), ((), ()))
TN = (((0,), (0,)), ((), ()))


def iota(shape, dim):
    return lax.broadcasted_iota(jnp.int32, shape, dim)


def dot(a, b, dims=None):
    if dims is None:
        return jnp.dot(a, b, preferred_element_type=F32)
    return lax.dot_general(a, b, dims, preferred_element_type=F32)


def slots(first, second):
    count = first.shape[1]
    down, across = iota((count, count), 0), iota((count, count), 1)
    eye = down == across
    earlier = (down < across).astype(F32)
    first_col = jnp.sum(jnp.where(eye, first, 0), axis=1, keepdims=True)
    second_col = jnp.sum(jnp.where(eye, second, 0), axis=1, keepdims=True)

    def total(hits):
        return jnp.sum(hits, axis=0, keepdims=True)

    rank_first = total((first_col == first).astype(F32) * earlier)
    rank_second = total((first_col == second).astype(F32)) + total(
        (second_col == second).astype(F32) * earlier
    )
    return (first, rank_first.astype(jnp.int32)), (second, rank_second.astype(jnp.int32))


def row_of(route):
    return route[0] * ROWS + route[1]


def rest_of(route):
    late = (route[1] >= 3).astype(jnp.int32)
    return route[0] * ROWS + CAP + late, route[1] - 3 * late


def chosen(hit_of, routes, shares):
    return sum(
        jnp.where(hit_of(route), share, 0.0) for route, share in zip(routes, shares)
    ).astype(BF16)


def packed_block(down, part, mine, last):
    def hit_of(route):
        row, column = rest_of(route)
        return (down == row) & (column == part)

    main = chosen(lambda route: down == row_of(route), mine[0], mine[1])
    left = jnp.concatenate([main, chosen(hit_of, last[0], last[1])], axis=1)
    return dot(left, jnp.concatenate([mine[2], last[2]], axis=0)).astype(BF16)


def block_at(place_ref, ref, delta):
    block = ref.shape[1] // 4
    start = lax.rem(place_ref[0] + delta, 4) * block
    return ref[:, pl.ds(pl.multiple_of(start, 128), block)]


def token_body(place_ref, ids_ref, values_ref, out_ref):
    count, width = values_ref.shape
    block = width // 4
    down = iota((out_ref.shape[0], count), 0)
    routes = slots(ids_ref[0:1, :], ids_ref[1:2, :])
    shares = (1.0, 1.0)
    last = (routes, shares, block_at(place_ref, values_ref, 3))
    for part in range(3):
        mine = (routes, shares, block_at(place_ref, values_ref, part))
        out_ref[:, part * block : (part + 1) * block] = packed_block(down, part, mine, last)


def dispatch_tokens(place, ids, values, experts):
    count, width = values.shape
    rows_all = experts * ROWS
    packed = 3 * width // 4
    spec = pl.BlockSpec(memory_space=pltpu.VMEM)
    return pl.pallas_call(
        token_body,
        out_shape=jax.ShapeDtypeStruct((rows_all, packed), BF16),
        in_specs=[pl.BlockSpec(memory_space=pltpu.SMEM), spec, spec],
        out_specs=spec,
        compiler_params=vmem(60),
        cost_estimate=pl.CostEstimate(
            flops=4 * rows_all * count * packed,
            bytes_accessed=2 * (count * width + rows_all * packed),
            transcendentals=0,
        ),
    )(place, ids, values)


NOTES = 16


def slice_body(place_ref, ids_ref, weight_ref, values_ref, *out_refs):
    count, width = values_ref.shape
    block = width // 4
    row = iota((NOTES, count), 0)
    notes = jnp.zeros((NOTES, count), F32)
    for k in range(2):
        notes = jnp.where(row == k, ids_ref[k : k + 1, :].astype(F32), notes)
        notes = jnp.where(row == 2 + k, weight_ref[k : k + 1, :].astype(F32), notes)
    for delta, out_ref in enumerate(out_refs):
        out_ref[:count, :] = block_at(place_ref, values_ref, delta)
        out_ref[count:, :] = jnp.zeros((NOTES, block), BF16)
        out_ref[count:, :count] = notes.astype(BF16)


def slices(place, ids, weight, values):
    count, width = values.shape
    spec = pl.BlockSpec(memory_space=pltpu.VMEM)
    return pl.pallas_call(
        slice_body,
        out_shape=[jax.ShapeDtypeStruct((count + NOTES, width // 4), BF16)] * 4,
        in_specs=[pl.BlockSpec(memory_space=pltpu.SMEM), spec, spec, spec],
        out_specs=[spec] * 4,
        compiler_params=vmem(12),
        cost_estimate=pl.CostEstimate(
            flops=0, bytes_accessed=4 * count * width, transcendentals=0
        ),
    )(place, ids, weight, values)


def grad_body(s0, s1, s2, s3, out_ref):
    count = s0.shape[0] - NOTES
    block = s0.shape[1]
    down = iota((out_ref.shape[0], count), 0)
    groups = []
    for ref in (s0, s1, s2, s3):
        notes = ref[count:, :count].astype(F32)
        first, second = (notes[k : k + 1, :].astype(jnp.int32) for k in range(2))
        groups.append((slots(first, second), (notes[2:3, :], notes[3:4, :]), ref[:count, :]))
    for part in range(3):
        out_ref[:, part * block : (part + 1) * block] = packed_block(
            down, part, groups[part], groups[3]
        )


def dispatch_grads(parts, experts):
    count, block = parts[0].shape
    rows_all = experts * ROWS
    spec = pl.BlockSpec(memory_space=pltpu.VMEM)
    return pl.pallas_call(
        grad_body,
        out_shape=jax.ShapeDtypeStruct((rows_all, 3 * block), BF16),
        in_specs=[spec] * 4,
        out_specs=spec,
        compiler_params=vmem(16),
        cost_estimate=pl.CostEstimate(
            flops=12 * rows_all * count * block,
            bytes_accessed=2 * (4 * count + 3 * rows_all) * block,
            transcendentals=0,
        ),
    )(*parts)


def pickers(experts):
    rows, packed = experts * CAP, experts * ROWS
    at, column = iota((rows, packed), 0), iota((rows, packed), 1)
    expert = lax.shift_right_logical(at * 10923, 16)
    slot = at - expert * CAP
    late = (slot >= 3).astype(jnp.int32)
    main = (column == expert * ROWS + slot).astype(BF16)
    rest = [
        ((column == expert * ROWS + CAP + late) & (slot - 3 * late == part)).astype(BF16)
        for part in range(3)
    ]
    return main, rest


def packers(experts):
    rows, packed = experts * CAP, experts * ROWS
    at, column = iota((packed, rows), 1), iota((packed, rows), 0)
    expert = lax.shift_right_logical(at * 10923, 16)
    slot = at - expert * CAP
    late = (slot >= 3).astype(jnp.int32)
    main = (column == expert * ROWS + slot).astype(BF16)
    rest = [
        ((column == expert * ROWS + CAP + late) & (slot - 3 * late == part)).astype(BF16)
        for part in range(3)
    ]
    return main, rest


def group_size(rows_all):
    experts = rows_all // ROWS
    return min(32, experts)


def unpack(packed_ref, whole_refs):
    rows_all, packed = packed_ref.shape
    block = packed // 3
    size = group_size(rows_all)
    main, rest = pickers(size)
    for group in range(rows_all // (size * ROWS)):
        source = slice(group * size * ROWS, (group + 1) * size * ROWS)
        target = slice(group * size * CAP, (group + 1) * size * CAP)
        parts = [packed_ref[source, part * block : (part + 1) * block] for part in range(3)]
        for part in range(3):
            whole_refs[part][target, :] = dot(main, parts[part]).astype(BF16)
        whole_refs[3][target, :] = sum(dot(rest[part], parts[part]) for part in range(3)).astype(
            BF16
        )


def project_body(got_ref, down_ref, g0, g1, g2, g3, b0, b1, b2, b3):
    wholes = (g0, g1, g2, g3)
    unpack(got_ref, wholes)
    hidden_width = down_ref.shape[0]
    step = min(256, hidden_width)
    for j in range(hidden_width // step):
        at = slice(j * step, (j + 1) * step)
        weight = down_ref[at, :]
        for whole, out_ref in zip(wholes, (b0, b1, b2, b3)):
            out_ref[:, at] = dot(whole[...], weight, NT).astype(out_ref.dtype)


def project(got, down):
    rows_all, packed = got.shape
    rows = rows_all // ROWS * CAP
    block, hidden_width = packed // 3, down.shape[0]
    return pl.pallas_call(
        project_body,
        out_shape=[jax.ShapeDtypeStruct((rows, block), BF16)] * 4
        + [jax.ShapeDtypeStruct((rows, hidden_width), F32)]
        + [jax.ShapeDtypeStruct((rows, hidden_width), BF16)] * 3,
        in_specs=[pl.BlockSpec(memory_space=pltpu.VMEM)] * 2,
        out_specs=[pl.BlockSpec(memory_space=pltpu.VMEM)] * 8,
        compiler_params=vmem(60),
        cost_estimate=pl.CostEstimate(
            flops=10 * rows * block * hidden_width,
            bytes_accessed=12 * rows * (block + hidden_width),
            transcendentals=0,
        ),
    )(got, down)


def unpack_rows_body(got_ref, x0, x1, x2, x3):
    unpack(got_ref, (x0, x1, x2, x3))


def unpack_rows(got):
    rows_all, packed = got.shape
    size = group_size(rows_all)
    block = packed // 3
    return pl.pallas_call(
        unpack_rows_body,
        grid=(rows_all // (size * ROWS),),
        out_shape=[jax.ShapeDtypeStruct((rows_all // ROWS * CAP, block), BF16)] * 4,
        in_specs=[pl.BlockSpec((size * ROWS, packed), lambda i: (i, 0))],
        out_specs=[pl.BlockSpec((size * CAP, block), lambda i: (i, 0))] * 4,
        compiler_params=vmem(12),
        cost_estimate=pl.CostEstimate(
            flops=12 * rows_all * size * CAP * block,
            bytes_accessed=4 * rows_all * packed,
            transcendentals=0,
        ),
    )(got)


def expert_body(
    x0, x1, x2, x3, up0, up1, up2a, up2b, up3, b0, b1, b2, b3,
    hidden_out, hgrad_out, ret_out,
    w0, w1, w2, w3, p0, p1, p2, p3, hidden_ref, hgrad_ref, ret_ref, in_sems, row_sems, ret_sems,
):
    rows, hidden_width = hidden_ref.shape
    block = w0.shape[0]
    half = block // 2
    step = min(512, hidden_width)
    steps = hidden_width // step
    sources = (up0, up1, up2a, up2b, up3, b0, b1, b2, b3)
    places = (w0, w1, w2.at[:half, :], w2.at[half:, :], w3, p0, p1, p2, p3)

    def fetch(j):
        at = slice(j * step, (j + 1) * step)
        group = [
            pltpu.make_async_copy(source.at[:, at], place.at[:, at], in_sems.at[p, j])
            for p, (source, place) in enumerate(zip(sources, places))
        ]
        for copy in group:
            copy.start()
        return group

    fetched = [fetch(0)]
    leaving = []
    score = jnp.zeros((rows, 1), F32)
    for j in range(steps):
        at = slice(j * step, (j + 1) * step)
        if j + 1 < steps:
            fetched.append(fetch(j + 1))
        for copy in fetched[j]:
            copy.wait()
        pre_act = dot(x0[...], w0[:, at])
        pre_act += dot(x1[...], w1[:, at])
        pre_act += dot(x2[...], w2[:, at])
        pre_act += dot(x3[...], w3[:, at])
        back = p0[:, at] + p1[:, at].astype(F32) + p2[:, at].astype(F32) + p3[:, at].astype(F32)
        sigmoid_val = jax.nn.sigmoid(pre_act)
        hidden = (pre_act * sigmoid_val).astype(BF16)
        hidden_ref[:, at] = hidden
        slope = sigmoid_val * (1.0 + pre_act * (1.0 - sigmoid_val))
        hgrad_ref[:, at] = (back * slope).astype(BF16)
        score += jnp.sum(hidden.astype(F32) * back, axis=1, keepdims=True)
        for k, (ref, out) in enumerate(((hidden_ref, hidden_out), (hgrad_ref, hgrad_out))):
            leaving.append(pltpu.make_async_copy(ref.at[:, at], out.at[:, at], row_sems.at[k, j]))
            leaving[-1].start()

    size = group_size(ret_ref.shape[0])
    main, rest = packers(size)
    groups = [
        (slice(g * size * CAP, (g + 1) * size * CAP), slice(g * size * ROWS, (g + 1) * size * ROWS))
        for g in range(rows // (size * CAP))
    ]
    high = score.astype(BF16)
    low = (score - high.astype(F32)).astype(BF16)
    lane = iota((rows, 128), 1)
    extra = jnp.where(lane == 0, high.astype(F32), jnp.where(lane == 1, low.astype(F32), 0.0))
    extra = extra.astype(BF16)
    for source, target in groups:
        ret_ref[target, 3 * block :] = dot(main, extra[source]).astype(BF16)

    def leave(start, width, at):
        copy = pltpu.make_async_copy(
            ret_ref.at[:, start : start + width], ret_out.at[:, start : start + width], ret_sems.at[at]
        )
        copy.start()
        leaving.append(copy)

    leave(3 * block, 128, 0)
    whole = hgrad_ref[...]
    chunk = min(768, block)
    for n in range(block // chunk):
        at = slice(n * chunk, (n + 1) * chunk)
        last = dot(whole, w3[at, :], NT).astype(BF16)
        for part, weight in enumerate((w0, w1, w2)):
            here = dot(whole, weight[at, :], NT).astype(BF16)
            start = part * block + n * chunk
            for source, target in groups:
                ret_ref[target, start : start + chunk] = (
                    dot(main, here[source]) + dot(rest[part], last[source])
                ).astype(BF16)
            leave(start, chunk, 1 + 3 * n + part)
    for copy in leaving:
        copy.wait()


def expert(wholes, ups, backs, experts):
    rows, block = wholes[0].shape
    hidden_width = ups[0].shape[1]
    packed = (experts * ROWS, 3 * block + 128)
    steps, chunks = hidden_width // min(512, hidden_width), block // min(768, block)
    spec = pl.BlockSpec(memory_space=pltpu.VMEM)
    anywhere = pl.BlockSpec(memory_space=pl.ANY)
    return pl.pallas_call(
        expert_body,
        out_shape=[jax.ShapeDtypeStruct((rows, hidden_width), BF16)] * 2
        + [jax.ShapeDtypeStruct(packed, BF16)],
        in_specs=[spec] * 4 + [anywhere] * 9,
        out_specs=[anywhere] * 3,
        scratch_shapes=[pltpu.VMEM((block, hidden_width), BF16)] * 4
        + [pltpu.VMEM((rows, hidden_width), F32)]
        + [pltpu.VMEM((rows, hidden_width), BF16)] * 5
        + [pltpu.VMEM(packed, BF16)]
        + [
            pltpu.SemaphoreType.DMA((9, steps)),
            pltpu.SemaphoreType.DMA((2, steps)),
            pltpu.SemaphoreType.DMA((1 + 3 * chunks,)),
        ],
        compiler_params=vmem(63),
        cost_estimate=pl.CostEstimate(
            flops=20 * rows * block * hidden_width,
            bytes_accessed=24 * block * hidden_width,
            transcendentals=rows * hidden_width,
        ),
    )(*wholes, *ups, *backs)


def combine_body(place_ref, ids_ref, weight_ref, ret_ref, dtok_ref, droute_ref):
    rows_all = ret_ref.shape[0]
    count, width = dtok_ref.shape
    block = width // 4
    routes = slots(ids_ref[0:1, :], ids_ref[1:2, :])
    eye = iota((count, count), 0) == iota((count, count), 1)

    def col(row):
        return jnp.sum(jnp.where(eye, row, jnp.zeros_like(row)), axis=1, keepdims=True)

    across = iota((count, rows_all), 1)
    hits = [(across == col(row_of(route))).astype(BF16) for route in routes]
    main = hits[0] + hits[1]
    rests = [rest_of(route) for route in routes]
    rest_rows = [col(row) for row, _ in rests]
    rest_parts = [col(part) for _, part in rests]

    def put(delta, values):
        start = lax.rem(place_ref[0] + delta, 4) * block
        dtok_ref[:, pl.ds(pl.multiple_of(start, 128), block)] = values.astype(BF16)

    last = jnp.zeros((count, block), F32)
    for part in range(3):
        got = ret_ref[:, part * block : (part + 1) * block]
        put(part, dot(main, got))
        pick = sum(
            ((across == row) & (column == part)).astype(F32)
            for row, column in zip(rest_rows, rest_parts)
        ).astype(BF16)
        last += dot(pick, got)
    put(3, last)
    extra = ret_ref[:, 3 * block :]
    for k in range(2):
        pair = dot(hits[k], extra)
        score = pair[:, 0:1] + pair[:, 1:2]
        row = jnp.sum(jnp.where(eye, score, 0.0), axis=0, keepdims=True)
        droute_ref[k : k + 1, :] = (row / weight_ref[k : k + 1, :].astype(F32)).astype(BF16)


def combine(place, ids, weight, ret, count, width):
    spec = pl.BlockSpec(memory_space=pltpu.VMEM)
    return pl.pallas_call(
        combine_body,
        out_shape=[
            jax.ShapeDtypeStruct((count, width), BF16),
            jax.ShapeDtypeStruct((2, count), BF16),
        ],
        in_specs=[pl.BlockSpec(memory_space=pltpu.SMEM), spec, spec, spec],
        out_specs=[spec, spec],
        compiler_params=vmem(20),
        cost_estimate=pl.CostEstimate(
            flops=4 * ret.shape[0] * count * width,
            bytes_accessed=2 * (count * width + ret.size),
            transcendentals=0,
        ),
    )(place, ids, weight, ret)


def near_body(l0, l1, l3, r0, r1, r3, out_ref):
    step = min(256, out_ref.shape[0])

    def one(j, carry):
        at = pl.ds(pl.multiple_of(j * step, step), step)
        total = dot(l0[:, at], r0[...], TN)
        total += dot(l1[:, at], r1[...], TN)
        total += dot(l3[:, at], r3[...], TN)
        out_ref[at, :] = total
        return carry

    lax.fori_loop(0, out_ref.shape[0] // step, one, 0)


def outer_near(lefts, rights):
    rows, shape = lefts[0].shape[0], (lefts[0].shape[1], rights[0].shape[1])
    return pl.pallas_call(
        near_body,
        out_shape=jax.ShapeDtypeStruct(shape, F32),
        in_specs=[pl.BlockSpec(memory_space=pltpu.VMEM)] * 6,
        out_specs=pl.BlockSpec(memory_space=pltpu.VMEM),
        compiler_params=vmem(16),
        cost_estimate=pl.CostEstimate(
            flops=6 * rows * shape[0] * shape[1],
            bytes_accessed=6 * rows * sum(shape) + 4 * shape[0] * shape[1],
            transcendentals=0,
        ),
    )(*lefts, *rights)


def last_body(left_in_halves, total_ref, whole, first, second, out_ref):
    half = first.shape[0]
    step = min(256, out_ref.shape[0])

    def one(j, carry):
        at = pl.ds(pl.multiple_of(j * step, step), step)
        total = total_ref[at, :]
        if left_in_halves:
            total += dot(first[:, at], whole[:half, :], TN)
            total += dot(second[:, at], whole[half:, :], TN)
        else:
            total += dot(whole[:half, at], first[...], TN)
            total += dot(whole[half:, at], second[...], TN)
        out_ref[at, :] = total.astype(BF16)
        return carry

    lax.fori_loop(0, out_ref.shape[0] // step, one, 0)


def outer_last(left_in_halves, total, whole, first, second):
    return pl.pallas_call(
        functools.partial(last_body, left_in_halves),
        out_shape=jax.ShapeDtypeStruct(total.shape, BF16),
        in_specs=[pl.BlockSpec(memory_space=pltpu.VMEM)] * 4,
        out_specs=pl.BlockSpec(memory_space=pltpu.VMEM),
        compiler_params=vmem(16),
        cost_estimate=pl.CostEstimate(
            flops=2 * whole.shape[0] * total.shape[0] * total.shape[1],
            bytes_accessed=6 * total.size + 2 * whole.shape[0] * sum(total.shape),
            transcendentals=0,
        ),
    )(total, whole, first, second)


def shift(values, by):
    count = lax.axis_size("cross")
    return lax.ppermute(values, "cross", [(i, (i + by) % count) for i in range(count)])


def near(own):
    return own, shift(own, -1), shift(own, 1)


def far(pieces):
    own, after, before = pieces
    half = own.shape[0] // 2
    return own, after, shift(before[:half], 1), shift(after[half:], -1), before


def transpose(parts):
    return parts[0], shift(parts[3], -1), shift(parts[2], 2), shift(parts[1], 1)


def exchange(values, experts):
    blocks = values.reshape(experts, ROWS, values.shape[1])
    return lax.all_to_all(blocks, "expert", split_axis=0, concat_axis=0, tiled=True).reshape(
        values.shape
    )


def shards(tokens, route_ids, route_weight, cotangent, up_weight, down_weight):
    experts = lax.axis_size("expert")
    count, width = tokens.shape
    place = lax.axis_index("cross").astype(jnp.int32).reshape(1)
    ids, weight = route_ids.T, route_weight.T
    cot_slices = transpose(slices(place, ids, weight, cotangent))
    got_grad = exchange(dispatch_grads(cot_slices, experts), experts)
    ups_near = near(up_weight[0])
    sent_tokens = dispatch_tokens(place, ids, tokens, experts)
    sent_tokens, ups_near = lax.optimization_barrier((sent_tokens, ups_near))
    ups = far(ups_near)
    got_tokens = exchange(sent_tokens, experts)
    g0, g1, g2, g3, b0, b1, b2, b3 = project(got_grad, down_weight[0])
    backs = transpose((b0, b1, b2, b3))
    got_tokens, backs, ups = lax.optimization_barrier((got_tokens, backs, ups))
    wholes = unpack_rows(got_tokens)
    t1, t3 = shift(wholes[3], -1), shift(wholes[1], 1)
    hidden, hidden_grad, ret = expert(wholes, ups, backs, experts)
    ret, t1, t3 = lax.optimization_barrier((ret, t1, t3))
    back = exchange(ret, experts)
    h0, h1, h2a, h2b, h3 = far(near(hidden))
    h2a, h2b, far_tokens = lax.optimization_barrier((h2a, h2b, wholes[2]))
    t2 = shift(far_tokens, 2)
    down_near = outer_near((h0, h1, h3), (g0, g1, g3))
    grads_near, down_near = lax.optimization_barrier((near(hidden_grad), down_near))
    d0, d1, d2a, d2b, d3 = far(grads_near)
    up_near = outer_near((wholes[0], t1, t3), (d0, d1, d3))
    grad_down = outer_last(True, down_near, g2, h2a, h2b)
    back, grad_down, up_near = lax.optimization_barrier((back, grad_down, up_near))
    d_tokens, d_route = combine(place, ids, weight, back, count, width)
    up_near, d_tokens, d_route = lax.optimization_barrier((up_near, d_tokens, d_route))
    grad_up = outer_last(False, up_near, t2, d2a, d2b)
    return d_tokens, d_route.T, grad_up[None], grad_down[None]


def solution(mesh):
    rows = P(("expert", "cross"), None)
    ups, downs = P("expert", "cross", None), P("expert", None, "cross")
    return jax.shard_map(
        shards,
        mesh=mesh,
        in_specs=(rows, rows, rows, rows, ups, downs),
        out_specs=(rows, rows, ups, downs),
        check_vma=False,
    )
```
